256 devices in a mesh: frame: 64 (over x, z_lo, y), head: 4 (over z_hi, core).
Axes of the slice: x: 4, y: 4, z: 8 (z_hi: 2, z_lo: 4; z = z_hi * 4 + z_lo), core: 2. Of those that a mesh axis runs over, the one named last changes fastest.
Arguments:
- tokens_in: bfloat16 [32768, 1152], P(('frame', 'head')), may hold values from -8 to 8
- mod_shift: float32 [1152], replicated, may hold values from -3 to 3
- mod_scale: float32 [1152], replicated, may hold values from -3 to 3
- branch_gate: float32 [1152], replicated, may hold values from -4 to 4
- inproj: bfloat16 [1152, 3, 1152], P(None, None, 'head'), may hold values from -0.3 to 0.3
- outproj: bfloat16 [1152, 1152], P('head'), may hold values from -0.1875 to 0.1875
- norm_gain: float32 [2, 72], replicated, may hold values from 0.5 to 6
- grad_result: bfloat16 [32768, 1152], P(('frame', 'head')), may hold values from -24 to 24
Outputs:
- result: bfloat16 [32768, 1152], P(('frame', 'head'))
- grad_in: bfloat16 [32768, 1152], P(('frame', 'head'))
- grad_inproj: float32 [1152, 3, 1152], P('frame', None, 'head')
- grad_outproj: float32 [1152, 1152], P('head', 'frame')
The draws below stay inside these ranges and needn't reach their ends.
All inputs are finite; a program needn't handle non-finite values.
Results may differ from the reference program's by a relative error of at most 0.024.
The reference program's roundings to bfloat16 on the way (of `modulated`, `normed`, `probs`, `attended`, `grad_scaled`, `grad_attended`, `grad_normed` and `grad_projected`) count: a program that leaves them out, or rounds other values in their place, can miss the bound.
Values may be sent and summed in bfloat16 or wider, within the bound.
A program may use at most 64 MiB of HBM per device.

```python
import jax
import jax.numpy as jnp
from jax import lax

D = 1152
HD = 72
FRAMES = 64
PIX = 512
TOKENS = 32768
N_HEAD = 4


def draw_tokens_in(key, part):
    key = jax.random.fold_in(key, 11)
    first = jax.random.fold_in(key, 0)
    values = jax.random.normal(first, (TOKENS, D), jnp.float32)
    return jnp.clip(values, -8.0, 8.0).astype(jnp.bfloat16)


def draw_inproj(key, part):
    key = jax.random.fold_in(key, 23)
    first = jax.random.fold_in(key, 0)
    values = jax.random.normal(first, (D, 3, D), jnp.float32) / jnp.sqrt(jnp.float32(D))
    return jnp.clip(values, -0.296875, 0.296875).astype(jnp.bfloat16)


def draw_norm_gain(key, part):
    key = jax.random.fold_in(key, 37)
    values = jax.random.uniform(key, (2, HD), jnp.float32, 0.5, 3.0)
    return values


def raised(array, own_key, source, target, blocks, factor):
    def block_of(position):
        return (jnp.arange(array.shape[position]) // (array.shape[position] // blocks)).reshape((-1,) + (1,) * (array.ndim - 1 - position))

    near = jax.random.permutation(own_key, blocks)[block_of(target)]
    second = (block_of(target) + blocks // 2) % blocks
    return jnp.where((block_of(source) == near) | (block_of(source) == second), factor * array, array)


def level_of(own_key, shape, cuts, least, top_value):
    factor_of = 1.0
    for axis_at, parts in cuts:
        steps = jax.random.uniform(jax.random.fold_in(jax.random.fold_in(own_key, 6), axis_at), (parts,), jnp.float32, least / len(cuts), top_value / len(cuts))
        factor_of = factor_of * jnp.repeat(jnp.exp(steps), shape[axis_at] // parts).reshape((-1,) + (1,) * (len(shape) - 1 - axis_at))
    return factor_of


def noise(key, dims, scale, limit, cuts=(), kind=jnp.bfloat16):
    values = scale * jax.random.normal(key, dims, jnp.float32)
    if cuts:
        values = values * level_of(key, dims, cuts, -0.22, 0.18)
    return jnp.clip(values, -limit, limit).astype(kind)


def gaussian_with(stream_key, shape, deviation, most, cuts, heavy, held_as=jnp.bfloat16):
    drawn = deviation * jax.random.normal(stream_key, shape, jnp.float32)
    if cuts:
        drawn = drawn * level_of(stream_key, shape, cuts, -0.22, 0.18)
    return jnp.clip(raised(drawn, jax.random.fold_in(stream_key, 3), *heavy), -most, most).astype(held_as)


def setup_inputs(seed: int = 0) -> dict:
    key_of = jax.random.split(jax.random.key(seed), 9)
    return {
        "tokens_in": draw_tokens_in(jax.random.fold_in(key_of[8], 71), 0),
        "mod_shift": noise(key_of[1], (D,), 0.5, 3.0, (), jnp.float32),
        "mod_scale": noise(key_of[2], (D,), 0.5, 3.0, (), jnp.float32),
        "branch_gate": noise(key_of[3], (D,), 1.0, 4.0, (), jnp.float32),
        "inproj": draw_inproj(jax.random.fold_in(key_of[8], 71), 0),
        "outproj": noise(key_of[5], (D, D), D ** -0.5, 0.1875, ((0, 4),)),
        "norm_gain": draw_norm_gain(jax.random.fold_in(key_of[8], 71), 0),
        "grad_result": gaussian_with(key_of[7], (TOKENS, D), 1.0, 24.0, ((0, 256),), (0, 1, 128, 5.5)),
    }


def layer_modulate(field, mod_shift, mod_scale):
    mean = lax.optimization_barrier(jnp.mean(field, axis=-1, keepdims=True))
    centred = field - mean
    spread = lax.optimization_barrier(jnp.mean(centred * centred, axis=-1, keepdims=True))
    return centred * lax.rsqrt(spread + 1e-06) * (1.0 + mod_scale) + mod_shift

def qk_norm(projected, norm_gain):
    rows = projected.shape[0]
    width = projected.shape[2]
    split = projected.reshape(rows, 3, width // HD, HD)
    query = split[:, 0]
    key_part = split[:, 1]
    query = query * lax.rsqrt(lax.optimization_barrier(jnp.mean(query * query, axis=-1, keepdims=True)) + 1e-06) * norm_gain[0]
    key_part = key_part * lax.rsqrt(lax.optimization_barrier(jnp.mean(key_part * key_part, axis=-1, keepdims=True)) + 1e-06) * norm_gain[1]
    joined = jnp.stack([query, key_part, split[:, 2]], axis=1)
    return joined.reshape(rows, 3, width).astype(jnp.bfloat16)

def attend(pixel_heads):
    frames, pixels, three, width = pixel_heads.shape
    split = pixel_heads.reshape(frames, pixels, 3, width // HD, HD).astype(jnp.float32)
    query = split[:, :, 0]
    key_part = split[:, :, 1]
    value = split[:, :, 2]
    scores = jnp.einsum('fphd,gphd->phfg', query, key_part) / jnp.sqrt(jnp.float32(HD))
    peak = lax.optimization_barrier(jnp.max(scores, axis=-1, keepdims=True))
    weights = jnp.exp(scores - peak)
    probs = (weights / lax.optimization_barrier(jnp.sum(weights, axis=-1, keepdims=True))).astype(jnp.bfloat16)
    mixed = jnp.einsum('phfg,gphd->fphd', probs.astype(jnp.float32), value)
    return mixed.reshape(frames, pixels, width).astype(jnp.bfloat16)

def grouped_product(left, right, groups):
    width = left.shape[1] // groups
    total = jnp.zeros((left.shape[0], right.shape[1]), jnp.float32)
    for group in range(groups):
        term = jnp.dot(left[:, group * width:(group + 1) * width], right[group * width:(group + 1) * width], preferred_element_type=jnp.float32)
        rounded = lax.optimization_barrier(term.astype(jnp.bfloat16))
        total = total + rounded.astype(jnp.float32)
    return total

def reference(tokens_in, mod_shift, mod_scale, branch_gate, inproj, outproj, norm_gain, grad_result):
    tokens = tokens_in.shape[0]
    width = inproj.shape[2]
    inputs = tokens_in.astype(jnp.float32)
    modulated = layer_modulate(inputs, mod_shift, mod_scale).astype(jnp.bfloat16)
    in_matrix = inproj.reshape(inproj.shape[0], 3 * width)
    projected = jnp.dot(modulated, in_matrix, preferred_element_type=jnp.float32).reshape(tokens, 3, width)
    normed = qk_norm(projected, norm_gain)
    pixel_heads = normed.reshape(FRAMES, PIX, 3, width)
    attended = attend(pixel_heads).reshape(tokens, width)
    attn_out = grouped_product(attended, outproj, N_HEAD)
    result = (inputs + branch_gate * attn_out).astype(jnp.bfloat16)
    grad_scaled = (branch_gate * grad_result.astype(jnp.float32)).astype(jnp.bfloat16)
    grad_outproj = jnp.dot(attended.T, grad_scaled, preferred_element_type=jnp.float32)
    grad_attended = jnp.dot(grad_scaled, outproj.T, preferred_element_type=jnp.float32).astype(jnp.bfloat16)
    unused, attend_back = jax.vjp(attend, pixel_heads)
    grad_normed = attend_back(grad_attended.reshape(FRAMES, PIX, width))[0]
    unused, norm_back = jax.vjp(lambda field: qk_norm(field, norm_gain), projected)
    grad_projected = norm_back(grad_normed.reshape(tokens, 3, width))[0].astype(jnp.bfloat16)
    grad_flat = grad_projected.reshape(tokens, 3 * width)
    grad_inproj = jnp.dot(modulated.T, grad_flat, preferred_element_type=jnp.float32).reshape(inproj.shape[0], 3, width)
    group_width = width // N_HEAD
    grad_mod = jnp.zeros((tokens, tokens_in.shape[1]), jnp.float32)
    for group in range(N_HEAD):
        columns = slice(group * group_width, (group + 1) * group_width)
        left = grad_projected[:, :, columns].reshape(tokens, 3 * group_width)
        right = inproj[:, :, columns].reshape(inproj.shape[0], 3 * group_width)
        term = jnp.dot(left, right.T, preferred_element_type=jnp.float32)
        rounded = lax.optimization_barrier(term.astype(jnp.bfloat16))
        grad_mod = grad_mod + rounded.astype(jnp.float32)
    unused, layer_back = jax.vjp(lambda field: layer_modulate(field, mod_shift, mod_scale), inputs)
    grad_layer = layer_back(grad_mod)[0]
    grad_in = (grad_result.astype(jnp.float32) + grad_layer).astype(jnp.bfloat16)
    return (result, grad_in, grad_inproj, grad_outproj)
```

```python
import functools

import jax
import jax.numpy as jnp
import ml_dtypes
import numpy as np
from jax import lax
from jax.experimental import pallas as pl
from jax.experimental.pallas import tpu as pltpu
from jax.sharding import PartitionSpec as P

D = 1152
HD = 72
W2 = 640
HW = 384
BF = jnp.bfloat16
F32 = jnp.float32
MESH = pl.DeviceIdType.MESH

STAGE1 = [(0, dz, dh, 0, 0, 0) for dz in range(4) for dh in range(2)]
STAGE2 = [(dx, 0, 0, dl, 0, 0) for dx in range(4) for dl in range(2)]
CORE = (0, 0, 0, 0, 0, 1)
ZHI = (0, 0, 0, 0, 1, 0)
XS = [(dx, 0, 0, 0, 0, 0) for dx in (1, 2, 3)]
YS = [(0, 0, dh, dl, 0, 0) for dh, dl in ((0, 1), (1, 0), (1, 1))]
ZSAME = [(0, dz, 0, 0, 0, 0) for dz in (1, 2, 3)]
ZOTHER = [(0, dz, 0, 0, 1, 0) for dz in range(4)]
PARTNERS = []
for _off in STAGE1[1:] + STAGE2[1:] + [CORE] + XS + YS + ZSAME + ZOTHER:
    if _off not in PARTNERS:
        PARTNERS.append(_off)


def one_hot(rows, cols, source):
    made = np.zeros((rows, cols), np.float32)
    for row in range(rows):
        col = source(row)
        if col is not None:
            made[row, col] = 1.0
    return made.astype(ml_dtypes.bfloat16)


def constants():
    swap = one_hot(128, 128, lambda o: (o // 2 % 8) * 16 + (o // 16) * 2 + o % 2)
    turn = one_hot(
        D, D, lambda t: (t % 288 // 72) * 288 + (t % 72 // 18) * 72 + (t // 288) * 18 + t % 18
    )
    first = one_hot(
        320,
        288,
        lambda o: (o % 80 // 18) * 72 + (o // 80) * 18 + o % 80 % 18 if o % 80 < 72 else None,
    )
    second = one_hot(320, 288, lambda o: (o // 80) * 72 + o % 80 if o % 80 < 72 else None)
    upper = one_hot(192, 80, lambda o: (o // 48) * 18 + o % 48 if o % 48 < 18 else None)
    lower = one_hot(
        192, 80, lambda o: (o // 48) * 18 + o % 48 - 18 if 18 <= o % 48 < 36 else None
    )
    heads = np.zeros((HW, HW), np.float32)
    for h in range(4):
        heads[h * HD : (h + 1) * HD, h * HD : (h + 1) * HD] = 1.0
    return (swap, turn, first, second, upper, lower, heads.astype(ml_dtypes.bfloat16))


def mm(a, b):
    return jnp.dot(a, b, preferred_element_type=F32)


def mm_nt(a, b):
    return lax.dot_general(a, b, (((1,), (1,)), ((), ())), preferred_element_type=F32)


def mm_tn(a, b):
    return lax.dot_general(a, b, (((0,), (0,)), ((), ())), preferred_element_type=F32)


def head_sum(values, ones):
    high = values.astype(BF)
    low = (values - high.astype(F32)).astype(BF)
    return mm(high, ones) + mm(low, ones)


def kernel(
    tok, grd, shift, scale, gate, gains, wa, swap, turn_hbm, first, second, upper, lower,
    heads,
    res_out, gin_out, sum_out,
    turn, wo, r1, per, full, mod, mod_t, both_t, gs, xf, yf, xn, kn, ga, rq, rk,
    acc_o, acc_q, acc_k, acc_v, ao, gm, gx, g1, g2, s1, s2, q1, zb, zr, cs, cr, ob, back, backp, fin,
    local_sem, ssem, rsem,
):
    f = lax.axis_index("frame")
    h = lax.axis_index("head")
    x, z, yh, yl = f // 16, (f // 4) % 4, (f // 2) % 2, f % 2
    zh, c = h // 2, h % 2
    y = yh * 2 + yl

    def coords(off):
        return (
            (x + off[0]) % 4,
            (z + off[1]) % 4,
            (yh + off[2]) % 2,
            (yl + off[3]) % 2,
            (zh + off[4]) % 2,
            (c + off[5]) % 2,
        )

    def dev(off):
        px, pz, ph, pw, pzh, pc = coords(off)
        return ((px * 4 + pz) * 4 + ph * 2 + pw, pzh * 2 + pc)

    count = [0]
    started = []

    def send(src, dst, off):
        at = count[0]
        count[0] += 1
        copy = pltpu.make_async_remote_copy(
            src_ref=src, dst_ref=dst, send_sem=ssem.at[at], recv_sem=rsem.at[at],
            device_id=dev(off), device_id_type=MESH,
        )
        copy.start()
        started.append(copy)
        return copy

    def rows(start, size):
        return pl.ds(pl.multiple_of(start, 16), size)

    load_turn = pltpu.make_async_copy(turn_hbm, turn, local_sem.at[0])
    load_turn.start()

    barrier = pltpu.get_barrier_semaphore()
    for off in PARTNERS:
        pl.semaphore_signal(barrier, inc=1, device_id=dev(off), device_id_type=MESH)
    pl.semaphore_wait(barrier, len(PARTNERS))

    def piece(px, py):
        return py % 2, (px * 2 + py // 2) * 144

    part, start = piece(x, y)
    w_z = send(wa.at[part, rows(start, 144)], wo.at[part, rows(start, 144)], ZHI)

    def stage1(src, which):
        out = []
        for slot, off in enumerate(STAGE1):
            _, pz, ph, _, _, _ = coords(off)
            block = rows((pz * 2 + ph) * 16, 16)
            if slot == 0:
                r1[which, 0:16, :] = src[block, :]
            else:
                out.append(send(src.at[block], r1.at[which, pl.ds(slot * 16, 16)], off))
        return out

    def stage2(which):
        per[which] = mm(swap[...], r1[which]).astype(BF)
        out = []
        for slot, off in enumerate(STAGE2):
            px, _, _, pw, _, _ = coords(off)
            block = rows((px * 2 + pw) * 16, 16)
            if slot == 0:
                full[which, 0:16, :] = per[which, block, :]
            else:
                out.append(
                    send(per.at[which, block], full.at[which, pl.ds(slot * 16, 16)], off)
                )
        return out

    def to_core(which):
        return send(full.at[which, pl.ds(0, 128)], full.at[which, pl.ds(128, 128)], CORE)

    def arrived(copies):
        for copy in copies:
            copy.wait_recv()

    tok1 = stage1(tok, 0)
    grd1 = stage1(grd, 1)

    w_z.wait_recv()
    w_x1 = [send(wo.at[part, rows(start, 80)], wo.at[part, rows(start, 80)], off) for off in XS]
    w_y1 = [
        send(wo.at[part, rows(start + 80, 64)], wo.at[part, rows(start + 80, 64)], off)
        for off in YS
    ]
    w_last = [send(wo.at[part, rows(start, 80)], wo.at[part, rows(start, 80)], off) for off in YS]
    w_last += [
        send(wo.at[part, rows(start + 80, 64)], wo.at[part, rows(start + 80, 64)], off)
        for off in XS
    ]

    arrived(tok1)
    tok2 = stage2(0)

    for copy, off in zip(w_x1, XS):
        copy.wait_recv()
        p2, st2 = piece((x - off[0]) % 4, y)
        w_last += [
            send(wo.at[p2, rows(st2, 80)], wo.at[p2, rows(st2, 80)], other) for other in YS
        ]
    for copy, off in zip(w_y1, YS):
        copy.wait_recv()
        p2, st2 = piece(x, ((yh + off[2]) % 2) * 2 + (yl + off[3]) % 2)
        w_last += [
            send(wo.at[p2, rows(st2 + 80, 64)], wo.at[p2, rows(st2 + 80, 64)], other)
            for other in XS
        ]

    arrived(tok2)
    tok3 = to_core(0)
    arrived(grd1)
    grd2 = stage2(1)
    load_turn.wait()
    tok3.wait_recv()

    def modulate(i, carry):
        at = pl.ds(pl.multiple_of(i * 32, 32), 32)
        field = full[0, at, :].astype(F32)
        mean = jnp.mean(field, axis=-1, keepdims=True)
        centred = field - mean
        spread = jnp.mean(centred * centred, axis=-1, keepdims=True)
        mod[at, :] = (
            centred * lax.rsqrt(spread + 1e-06) * (1.0 + scale[...]) + shift[...]
        ).astype(BF)
        return carry

    lax.fori_loop(0, 8, modulate, 0)
    mod_t[...] = mod[...].T
    both_t[:, 0:256] = mm(turn[...], mod_t[...]).astype(BF)

    lane = lax.broadcasted_iota(jnp.int32, (1, HW), 1)
    row_i = lax.broadcasted_iota(jnp.int32, (256, 256), 0)
    col_i = lax.broadcasted_iota(jnp.int32, (256, 256), 1)
    gain_q = gains[0:1, :]
    gain_k = gains[1:2, :]

    def forward(w):
        xf[...] = mm(mod[...], w[0])
        yf[...] = mm(mod[...], w[1, :, 0:HW])
        q = xf[:, 0:HW]
        q = jnp.where(lane < 288, q, 0.0)
        r = lax.rsqrt(head_sum(q * q, heads[...]) * (1.0 / HD) + 1e-06)
        rq[...] = r
        qn = jnp.where(lane < 288, q * r * gain_q, xf[:, 0:HW])
        xn[:, 0:HW] = qn.astype(BF)
        xn[:, HW:W2] = xf[:, HW:W2].astype(BF)
        k = jnp.where(lane < 288, yf[...], 0.0)
        r = lax.rsqrt(head_sum(k * k, heads[...]) * (1.0 / HD) + 1e-06)
        rk[...] = r
        kn[...] = (k * r * gain_k).astype(BF)

    def attention():
        acc_o[...] = jnp.zeros_like(acc_o)
        acc_q[...] = jnp.zeros_like(acc_q)
        acc_k[...] = jnp.zeros_like(acc_k)
        acc_v[...] = jnp.zeros_like(acc_v)
        same = (row_i // 128 == col_i // 128) & (row_i % 2 == col_i % 2)
        root = 1.0 / np.sqrt(np.float32(HD))

        def head(i, carry):
            in_q = (lane >= i * HD) & (lane < i * HD + HD)
            in_v = (lane >= i * HD + 32) & (lane < i * HD + 32 + HD)
            zero = jnp.zeros((), BF)
            qh = jnp.where(in_q, xn[:, 0:HW], zero)
            kh = jnp.where(in_q, kn[...], zero)
            vh = jnp.where(in_v, xn[:, 256:W2], zero)
            gh = jnp.where(in_v, ga[...], zero)
            s = jnp.where(same, mm_nt(qh, kh) * root, -1e30)
            e = jnp.exp(s - jnp.max(s, axis=-1, keepdims=True))
            p = e * (1.0 / jnp.sum(e, axis=-1, keepdims=True))
            pb = p.astype(BF)
            acc_o[...] += mm(pb, vh)
            acc_v[...] += mm_tn(pb, gh)
            dp = mm_nt(gh, vh)
            ds = (p * (dp - jnp.sum(p * dp, axis=-1, keepdims=True)) * root).astype(BF)
            acc_q[...] += mm(ds, kh)
            acc_k[...] += mm_tn(ds, qh)
            return carry

        lax.fori_loop(0, 4, head, 0)

    def unnorm(cot, raw, r, gain):
        n = jnp.where(lane < 288, raw * r, 0.0)
        dn = cot.astype(BF).astype(F32) * gain
        inner = head_sum(n * dn, heads[...]) * (1.0 / HD)
        return jnp.where(lane < 288, r * (dn - n * inner), 0.0).astype(BF)

    def backward(g, w):
        gq = unnorm(acc_q[...], xf[:, 0:HW], rq[...], gain_q)
        gk = unnorm(acc_k[...], yf[...], rk[...], gain_k)
        gv = acc_v[...].astype(BF)
        att = acc_o[...].astype(BF)
        gx[0:256, 0:256] = gq[:, 0:256]
        gx[0:256, 256:HW] = gq[:, 256:HW] + gv[:, 0:128]
        gx[0:256, HW:W2] = gv[:, 128:HW]
        gx[256:512, 0:HW] = gk
        gx[256:512, HW:W2] = jnp.zeros((256, W2 - HW), BF)
        gx[512:768, 0:256] = jnp.zeros((256, 256), BF)
        gx[512:768, 256:W2] = att

        def grads(i, carry):
            at = pl.ds(pl.multiple_of(i * 288, 288), 288)
            g1[g, at, :] = mm(mod_t[at, :], gx[0:256, :]).astype(BF)
            g2[g, at, :] = mm(both_t[at, :], gx[256:768, :]).astype(BF)
            return carry

        lax.fori_loop(0, 4, grads, 0)
        out = mm_nt(gx[512:768, 256:W2], w[1, :, 256:W2])
        back_mod = mm_nt(gx[0:256, :], w[0]) + mm_nt(gx[256:512, 0:HW], w[1, :, 0:HW])
        if g == 0:
            ao[...] = out
            gm[...] = back_mod
        else:
            ao[...] += out
            gm[...] += back_mod

    def reduce_first(g):
        a, b = [], []
        for i, off in enumerate(XS):
            px = coords(off)[0]
            a.append(send(g1.at[g, rows(px * 288, 288)], s1.at[g, 0, i], off))
        for i, off in enumerate(YS):
            _, _, ph, pw, _, _ = coords(off)
            b.append(send(g2.at[g, rows((ph * 2 + pw) * 288, 288)], s1.at[g, 1, i], off))
        return a, b

    def reduce_second(g, copies):
        out = []
        for half, (grad, at, spread, offs) in enumerate(
            ((g1, x, first, YS), (g2, y, second, XS))
        ):
            arrived(copies[half])
            total = grad[g, rows(at * 288, 288), :].astype(F32)
            for i in range(3):
                total = total + s1[g, half, i].astype(F32)
            q1[g, half] = mm(spread[...], total.astype(BF)).astype(BF)
            sent = []
            for i, off in enumerate(offs):
                px, _, ph, pw, _, _ = coords(off)
                to = ph * 2 + pw if half == 0 else px
                sent.append(send(q1.at[g, half, rows(to * 80, 80)], s2.at[g, half, i], off))
            out.append(sent)
        return out

    def reduce_z(g, copies):
        sums = []
        for half, at in ((0, y), (1, x)):
            arrived(copies[half])
            total = q1[g, half, rows(at * 80, 80), :].astype(F32)
            for i in range(3):
                total = total + s2[g, half, i].astype(F32)
            sums.append(total.astype(BF))
        zb[g] = (mm(upper[...], sums[0]) + mm(lower[...], sums[1])).astype(BF)
        out = []
        for off in ZSAME if g == 0 else ZOTHER:
            slot = off[1] - 1 if g == 0 else 3 + off[1]
            pz = coords(off)[1]
            out.append(send(zb.at[g, rows(pz * 48, 48)], zr.at[slot], off))
        return out

    forward(wa)
    arrived(grd2)
    grd3 = to_core(1)
    grd3.wait_recv()
    gs[...] = (full[1].astype(F32) * gate[...]).astype(BF)
    mod_t2 = gs[...].T
    both_t[:, 256:512] = mm(turn[...], mod_t2).astype(BF)

    def cotangent(w):
        raw = mm(gs[...], w[1, :, 256:W2])
        ga[...] = jnp.where((lane >= 32) & (lane < 320), raw, 0.0).astype(BF)

    cotangent(wa)
    attention()
    backward(0, wa)
    sum_a = reduce_first(0)
    arrived(w_last)
    forward(wo)
    cotangent(wo)
    attention()
    backward(1, wo)
    sum_b = reduce_first(1)

    cs[0] = ao[128:256, :].astype(BF)
    cs[1] = gm[128:256, :].astype(BF)
    shares = [send(cs.at[i], cr.at[i], CORE) for i in range(2)]

    def back_stage2(which):
        out = []
        for slot, off in enumerate(STAGE2):
            inv = tuple(-v for v in off)
            block = rows((x * 2 + yl) * 16, 16)
            if slot == 0:
                back[which, block, :] = ob[which, 0:16, :]
            else:
                out.append(send(ob.at[which, pl.ds(slot * 16, 16)], back.at[which, block], inv))
        return out

    def back_stage1(which):
        backp[which] = mm(swap[...], back[which]).astype(BF)
        out = []
        for slot, off in enumerate(STAGE1):
            inv = tuple(-v for v in off)
            block = rows((z * 2 + yh) * 16, 16)
            if slot == 0:
                fin[which, block, :] = backp[which, 0:16, :]
            else:
                out.append(send(backp.at[which, pl.ds(slot * 16, 16)], fin.at[which, block], inv))
        return out

    shares[0].wait_recv()
    ob[0] = (
        full[0, 0:128, :].astype(F32) + gate[...] * (ao[0:128, :] + cr[0].astype(F32))
    ).astype(BF)
    res2 = back_stage2(0)
    shares[1].wait_recv()

    def layer_back(i, carry):
        at = pl.ds(pl.multiple_of(i * 32, 32), 32)
        field = full[0, at, :].astype(F32)
        mean = jnp.mean(field, axis=-1, keepdims=True)
        centred = field - mean
        spread = jnp.mean(centred * centred, axis=-1, keepdims=True)
        r = lax.rsqrt(spread + 1e-06)
        hat = centred * r
        d = (gm[at, :] + cr[1, at, :].astype(F32)) * (1.0 + scale[...])
        dx = r * (
            d
            - jnp.mean(d, axis=-1, keepdims=True)
            - hat * jnp.mean(d * hat, axis=-1, keepdims=True)
        )
        ob[1, at, :] = (full[1, at, :].astype(F32) + dx).astype(BF)
        return carry

    lax.fori_loop(0, 4, layer_back, 0)
    gin2 = back_stage2(1)

    sum_a = reduce_second(0, sum_a)
    arrived(res2)
    res1 = back_stage1(0)
    arrived(gin2)
    gin1 = back_stage1(1)
    sum_a = reduce_z(0, sum_a)
    sum_b = reduce_second(1, sum_b)
    arrived(res1)
    res_out[...] = fin[0]
    arrived(gin1)
    gin_out[...] = fin[1]
    sum_b = reduce_z(1, sum_b)
    arrived(sum_a)
    arrived(sum_b)
    total = zb[0, rows(z * 48, 48), :].astype(F32)
    for i in range(7):
        total = total + zr[i].astype(F32)
    sum_out[...] = total
    for copy in started:
        copy.wait_send()


N_COPY = 1 + 14 + 6 + 6 + 18 + 14 + 2 + 12 + 12 + 7 + 2 + 14 + 14


def body(tokens_in, mod_shift, mod_scale, branch_gate, inproj, outproj, norm_gain, grad_result):
    pad = jnp.zeros((D, W2 - 576), BF)
    weights = jnp.stack(
        [
            jnp.concatenate([inproj[:, 0], inproj[:, 2], pad], axis=1),
            jnp.concatenate([inproj[:, 1], outproj.T, pad], axis=1),
        ]
    )
    gains = jnp.pad(jnp.tile(norm_gain, (1, 4)), ((0, 0), (0, HW - 288)))
    swap, turn, first, second, upper, lower, heads = constants()
    vm = pl.BlockSpec(memory_space=pltpu.VMEM)
    anys = pl.BlockSpec(memory_space=pl.ANY)

    def vmem(shape, dtype=BF):
        return pltpu.VMEM(shape, dtype)

    result, grad_in, summed = pl.pallas_call(
        kernel,
        out_shape=(
            jax.ShapeDtypeStruct((128, D), BF),
            jax.ShapeDtypeStruct((128, D), BF),
            jax.ShapeDtypeStruct((48, W2), F32),
        ),
        in_specs=[vm] * 7 + [vm, anys] + [vm] * 5,
        out_specs=(vm, vm, vm),
        scratch_shapes=[
            vmem((D, D)),
            vmem((2, D, W2)),
            vmem((2, 128, D)),
            vmem((2, 128, D)),
            vmem((2, 256, D)),
            vmem((256, D)),
            vmem((D, 256)),
            vmem((D, 512)),
            vmem((256, D)),
            vmem((256, W2), F32),
            vmem((256, HW), F32),
            vmem((256, W2)),
            vmem((256, HW)),
            vmem((256, HW)),
            vmem((256, HW), F32),
            vmem((256, HW), F32),
            vmem((256, HW), F32),
            vmem((256, HW), F32),
            vmem((256, HW), F32),
            vmem((256, HW), F32),
            vmem((256, D), F32),
            vmem((256, D), F32),
            vmem((768, W2)),
            vmem((2, D, W2)),
            vmem((2, D, W2)),
            vmem((2, 2, 3, 288, W2)),
            vmem((2, 2, 3, 80, W2)),
            vmem((2, 2, 320, W2)),
            vmem((2, 192, W2)),
            vmem((7, 48, W2)),
            vmem((2, 128, D)),
            vmem((2, 128, D)),
            vmem((2, 128, D)),
            vmem((2, 128, D)),
            vmem((2, 128, D)),
            vmem((2, 128, D)),
            pltpu.SemaphoreType.DMA((1,)),
            pltpu.SemaphoreType.DMA((N_COPY,)),
            pltpu.SemaphoreType.DMA((N_COPY,)),
        ],
        compiler_params=pltpu.CompilerParams(
            collective_id=0, has_side_effects=True, vmem_limit_bytes=58 * 2**20
        ),
        name="sublayer",
    )(
        tokens_in, grad_result, mod_shift[None], mod_scale[None], branch_gate[None], gains,
        weights, swap, turn, first, second, upper, lower, heads,
    )
    grad_inproj = jnp.stack(
        [summed[0:18, 0:288], summed[18:36, 0:288], summed[0:18, 288:576]], axis=1
    )
    return result, grad_in, grad_inproj, summed[18:36, 288:576].T


def solution(mesh):
    placed = (
        P(("frame", "head"), None),
        P(),
        P(),
        P(),
        P(None, None, "head"),
        P("head", None),
        P(),
        P(("frame", "head"), None),
    )
    return jax.shard_map(
        body,
        mesh=mesh,
        in_specs=placed,
        out_specs=(
            P(("frame", "head"), None),
            P(("frame", "head"), None),
            P("frame", None, "head"),
            P("head", "frame"),
        ),
        check_vma=False,
    )
```

```python
import functools

import jax
import jax.numpy as jnp
import ml_dtypes
import numpy as np
from jax import lax
from jax.experimental import pallas as pl
from jax.experimental.pallas import tpu as pltpu
from jax.sharding import PartitionSpec as P

D = 1152
HD = 72
W2 = 640
W1 = D - W2
HC = 288
BF = jnp.bfloat16
F32 = jnp.float32
MESH = pl.DeviceIdType.MESH

def one_hot(rows, cols, source):
    made = np.zeros((rows, cols), np.float32)
    for row in range(rows):
        col = source(row)
        if col is not None:
            made[row, col] = 1.0
    return made.astype(ml_dtypes.bfloat16)


def constants():
    swap = one_hot(128, 128, lambda o: (o // 2 % 8) * 16 + (o // 16) * 2 + o % 2)
    turn = one_hot(
        D, D, lambda t: (t % 288 // 72) * 288 + (t % 72 // 18) * 72 + (t // 288) * 18 + t % 18
    )
    first = one_hot(
        320,
        288,
        lambda o: (o % 80 // 18) * 72 + (o // 80) * 18 + o % 80 % 18 if o % 80 < 72 else None,
    )
    second = one_hot(320, 288, lambda o: (o // 80) * 72 + o % 80 if o % 80 < 72 else None)
    upper = one_hot(192, 80, lambda o: (o // 48) * 18 + o % 48 if o % 48 < 18 else None)
    lower = one_hot(
        192, 80, lambda o: (o // 48) * 18 + o % 48 - 18 if 18 <= o % 48 < 36 else None
    )
    heads = np.zeros((HC, HC), np.float32)
    for h in range(4):
        heads[h * HD : (h + 1) * HD, h * HD : (h + 1) * HD] = 1.0
    return (swap, turn, first, second, upper, lower, heads.astype(ml_dtypes.bfloat16))


def mm(a, b):
    return jnp.dot(a, b, preferred_element_type=F32)


def mm_nt(a, b):
    return lax.dot_general(a, b, (((1,), (1,)), ((), ())), preferred_element_type=F32)


def mm_tn(a, b):
    return lax.dot_general(a, b, (((0,), (0,)), ((), ())), preferred_element_type=F32)


def head_sum(values, ones):
    high = values.astype(BF)
    low = (values - high.astype(F32)).astype(BF)
    return mm(high, ones) + mm(low, ones)


def kernel(
    tok, grd, shift_in, scale_in, gate_in, gain_in, w_in, w_out, swap, turn_hbm, first, second,
    upper, lower, heads,
    res_out, gin_out, inproj_out, outproj_out,
    wown, turn, wo, r1, per, full, mod, mod_t, both_t, gs, qf, kf, qn, kn, vn, ga, rq, rk,
    acc_o, acc_q, acc_k, acc_v, ao, gm, gx1, gx2, g1, g2, m1, s1, q1, m2, s2, zb, zr, cs, cr,
    ob, back, backp, fin,
    local_sem, ssem, rsem,
):
    f = lax.axis_index("frame")
    h = lax.axis_index("head")
    x, z, yh, yl = f // 16, (f // 4) % 4, (f // 2) % 2, f % 2
    zh, c = h // 2, h % 2
    y = yh * 2 + yl

    def dev(px=x, pz=z, py=y, ph=zh, pc=c):
        return ((px * 4 + pz) * 4 + py, ph * 2 + pc)

    def flip(dh, dl):
        return ((yh + dh) % 2) * 2 + (yl + dl) % 2

    stage1_to = [dev(pz=(z + dz) % 4, py=flip(dh, 0)) for dz in range(4) for dh in range(2)]
    stage1_at = [((z + dz) % 4) * 2 + (yh + dh) % 2 for dz in range(4) for dh in range(2)]
    stage1_from = [dev(pz=(z - dz) % 4, py=flip(dh, 0)) for dz in range(4) for dh in range(2)]
    stage2_to = [dev(px=(x + dx) % 4, py=flip(0, dl)) for dx in range(4) for dl in range(2)]
    stage2_at = [((x + dx) % 4) * 2 + (yl + dl) % 2 for dx in range(4) for dl in range(2)]
    stage2_from = [dev(px=(x - dx) % 4, py=flip(0, dl)) for dx in range(4) for dl in range(2)]
    core = dev(pc=1 - c)
    mirror = dev(pz=3 - z, ph=1 - zh)
    z_other = [dev(pz=(z + dz) % 4, ph=1 - zh) for dz in range(4)]
    z_same = [dev(pz=(z + dz) % 4) for dz in (1, 2, 3)]
    partners = stage1_to[1:] + stage2_to[1:] + [dev(py=flip(1, 1)), core] + z_other

    count = [0]
    started = []

    def send(src, dst, to):
        at = count[0]
        count[0] += 1
        copy = pltpu.make_async_remote_copy(
            src_ref=src, dst_ref=dst, send_sem=ssem.at[at], recv_sem=rsem.at[at],
            device_id=to, device_id_type=MESH,
        )
        copy.start()
        started.append(copy)
        return copy

    def rows(start, size):
        return pl.ds(pl.multiple_of(start, 16), size)

    def arrived(copies):
        for copy in copies:
            copy.wait_recv()

    load_in = pltpu.make_async_copy(w_in, wown.at[pl.ds(0, 864)], local_sem.at[0])
    load_out = pltpu.make_async_copy(w_out, wown.at[pl.ds(864, HC)], local_sem.at[1])
    load_turn = pltpu.make_async_copy(turn_hbm, turn, local_sem.at[2])
    load_in.start()
    load_out.start()
    load_turn.start()

    barrier = pltpu.get_barrier_semaphore()
    for to in partners:
        pl.semaphore_signal(barrier, inc=1, device_id=to, device_id_type=MESH)
    pl.semaphore_wait(barrier, len(partners))

    def stage1(src, which):
        out = []
        for slot in range(8):
            block = rows(stage1_at[slot] * 16, 16)
            if slot == 0:
                r1[which, 0:16, :] = src[block, :]
            else:
                out.append(
                    send(src.at[block], r1.at[which, pl.ds(slot * 16, 16)], stage1_to[slot])
                )
        return out

    def stage2(which):
        per[which] = mm(swap[...], r1[which]).astype(BF)
        out = []
        for slot in range(8):
            block = rows(stage2_at[slot] * 16, 16)
            if slot == 0:
                full[which, 0:16, :] = per[which, block, :]
            else:
                out.append(
                    send(
                        per.at[which, block],
                        full.at[which, pl.ds(slot * 16, 16)],
                        stage2_to[slot],
                    )
                )
        return out

    def to_core(which):
        return send(full.at[which, pl.ds(0, 128)], full.at[which, pl.ds(128, 128)], core)

    tok1 = stage1(tok, 0)

    def piece(px, py):
        return py % 2, (px * 2 + py // 2) * 144

    part, start = piece(x, y)
    load_in.wait()
    load_out.wait()
    w_z = send(
        wown.at[rows(start, 144), pl.ds(pl.multiple_of(part * 512, 128), W2)],
        wo.at[part, rows(start, 144)],
        mirror,
    )
    grd1 = stage1(grd, 1)

    def over_x(pc, st):
        ref = wo.at[pc, rows(st + 80, 64)]
        return [send(ref, ref, dev(px=(x + dx) % 4)) for dx in (1, 2, 3)]

    def over_y(pc, st):
        ref = wo.at[pc, rows(st, 80)]
        return [send(ref, ref, dev(py=flip(*d))) for d in ((0, 1), (1, 0), (1, 1))]

    arrived(tok1)
    tok2 = stage2(0)
    w_z.wait_recv()
    first_x = wo.at[part, rows(start, 80)]
    w_x1 = [send(first_x, first_x, dev(px=(x + dx) % 4)) for dx in (1, 2, 3)]
    first_y = wo.at[part, rows(start + 80, 64)]
    w_y1 = [send(first_y, first_y, dev(py=flip(*d))) for d in ((0, 1), (1, 0), (1, 1))]
    w_last = over_y(part, start) + over_x(part, start)
    arrived(grd1)
    grd2 = stage2(1)
    arrived(tok2)
    tok3 = to_core(0)
    load_turn.wait()
    tok3.wait_recv()

    shift = shift_in[...].reshape(1, D)
    scale = scale_in[...].reshape(1, D)
    gate = gate_in[...].reshape(1, D)

    def modulate(i, carry):
        at = pl.ds(pl.multiple_of(i * 32, 32), 32)
        field = full[0, at, :].astype(F32)
        mean = jnp.mean(field, axis=-1, keepdims=True)
        centred = field - mean
        spread = jnp.mean(centred * centred, axis=-1, keepdims=True)
        mod[at, :] = (centred * lax.rsqrt(spread + 1e-06) * (1.0 + scale) + shift).astype(BF)
        return carry

    lax.fori_loop(0, 8, modulate, 0)

    for copy, dx in zip(w_x1, (1, 2, 3)):
        copy.wait_recv()
        w_last += over_y(*piece((x - dx) % 4, y))
    for copy, d in zip(w_y1, ((0, 1), (1, 0), (1, 1))):
        copy.wait_recv()
        w_last += over_x(*piece(x, flip(*d)))

    lane = lax.broadcasted_iota(jnp.int32, (1, HC), 1)
    row_i = lax.broadcasted_iota(jnp.int32, (256, 256), 0)
    col_i = lax.broadcasted_iota(jnp.int32, (256, 256), 1)
    gain_q = jnp.concatenate([gain_in[0:1, :]] * 4, axis=1)
    gain_k = jnp.concatenate([gain_in[1:2, :]] * 4, axis=1)

    def own(j):
        at = pl.ds(j * HC, HC)
        return wown[at, 0:W2], wown[at, W2:D]

    def other(j):
        at = pl.ds(j * HC, HC)
        return wo[0, at, :], wo[1, at, W2 - W1 : W2]

    def project(act, w, j):
        low, high = w(j)
        return mm_nt(act[:, 0:W2], low) + mm_nt(act[:, W2:D], high)

    def forward(w):
        q = project(mod, w, 0)
        qf[...] = q
        r = lax.rsqrt(head_sum(q * q, heads[...]) * (1.0 / HD) + 1e-06)
        rq[...] = r
        qn[...] = (q * r * gain_q).astype(BF)
        k = project(mod, w, 1)
        kf[...] = k
        r = lax.rsqrt(head_sum(k * k, heads[...]) * (1.0 / HD) + 1e-06)
        rk[...] = r
        kn[...] = (k * r * gain_k).astype(BF)
        vn[...] = project(mod, w, 2).astype(BF)

    def cotangent(w):
        ga[...] = project(gs, w, 3).astype(BF)

    def attention():
        acc_o[...] = jnp.zeros_like(acc_o)
        acc_q[...] = jnp.zeros_like(acc_q)
        acc_k[...] = jnp.zeros_like(acc_k)
        acc_v[...] = jnp.zeros_like(acc_v)
        same = (row_i // 128 == col_i // 128) & (row_i % 2 == col_i % 2)
        root = 1.0 / np.sqrt(np.float32(HD))

        def head(i, carry):
            inside = (lane >= i * HD) & (lane < i * HD + HD)
            zero = jnp.zeros((), BF)
            qh = jnp.where(inside, qn[...], zero)
            kh = jnp.where(inside, kn[...], zero)
            vh = jnp.where(inside, vn[...], zero)
            gh = jnp.where(inside, ga[...], zero)
            s = jnp.where(same, mm_nt(qh, kh) * root, -1e30)
            e = jnp.exp(s - jnp.max(s, axis=-1, keepdims=True))
            p = e * (1.0 / jnp.sum(e, axis=-1, keepdims=True))
            pb = p.astype(BF)
            acc_o[...] += mm(pb, vh)
            acc_v[...] += mm_tn(pb, gh)
            dp = mm_nt(gh, vh)
            ds = (p * (dp - jnp.sum(p * dp, axis=-1, keepdims=True)) * root).astype(BF)
            acc_q[...] += mm(ds, kh)
            acc_k[...] += mm_tn(ds, qh)
            return carry

        lax.fori_loop(0, 4, head, 0)

    def unnorm(cot, raw, r, gain):
        n = raw * r
        dn = cot.astype(BF).astype(F32) * gain
        inner = head_sum(n * dn, heads[...]) * (1.0 / HD)
        return (r * (dn - n * inner)).astype(BF)

    def grads(g):
        gq = unnorm(acc_q[...], qf[...], rq[...], gain_q)
        gk = unnorm(acc_k[...], kf[...], rk[...], gain_k)
        gv = acc_v[...].astype(BF)
        att = acc_o[...].astype(BF)
        pad = jnp.zeros((256, W2 - 2 * HC), BF)
        gx1[...] = jnp.concatenate([gq, gv, pad], axis=1)
        gx2[0:256, :] = jnp.concatenate([gk, jnp.zeros((256, W2 - HC), BF)], axis=1)
        gx2[256:512, :] = jnp.concatenate([jnp.zeros((256, HC), BF), att, pad], axis=1)

        def block(i, carry):
            at = pl.ds(pl.multiple_of(i * 288, 288), 288)
            g1[g, at, :] = mm(mod_t[at, :], gx1[...]).astype(BF)
            g2[g, at, :] = mm(both_t[at, :], gx2[...]).astype(BF)
            return carry

        lax.fori_loop(0, 4, block, 0)
        return gq, gk, gv, att

    def shares(g, w, parts):
        gq, gk, gv, att = parts
        (q0, q1_), (k0, k1_), (v0, v1_), (o0, o1_) = w(0), w(1), w(2), w(3)
        pieces = (
            (ao, pl.ds(0, W2), mm(att, o0)),
            (ao, pl.ds(W2, W1), mm(att, o1_)),
            (gm, pl.ds(0, W2), mm(gq, q0) + mm(gk, k0) + mm(gv, v0)),
            (gm, pl.ds(W2, W1), mm(gq, q1_) + mm(gk, k1_) + mm(gv, v1_)),
        )
        for ref, at, value in pieces:
            if g == 0:
                ref[:, at] = value
            else:
                ref[:, at] += value

    axes = (
        (x, dev(px=(x + 1) % 4), dev(px=(x - 1) % 4)),
        (y, dev(py=(y + 1) % 4), dev(py=(y - 1) % 4)),
    )

    def ring_start(ref, land, axis, size, cut):
        me, right, left = axes[axis]
        a = lambda k: ref.at[rows((me + k) % 4 * size, cut)]
        b = lambda k: ref.at[rows((me + k) % 4 * size + cut, size - cut)]
        top, low = pl.ds(0, cut), pl.ds(0, size - cut)
        return [
            send(a(2), land.at[0, top], right),
            send(b(2), land.at[1, low], left),
            send(b(1), land.at[2, low], right),
            send(a(3), land.at[3, top], left),
        ]

    def ring_middle(ref, land, merged, axis, size, cut, copies):
        me, right, left = axes[axis]
        top, low = pl.ds(0, cut), pl.ds(0, size - cut)
        copies[0].wait_recv()
        merged[0, top, :] = (
            ref[rows((me + 1) % 4 * size, cut), :].astype(F32) + land[0, top, :].astype(F32)
        ).astype(BF)
        out = [send(merged.at[0, top], land.at[4, top], right)]
        copies[1].wait_recv()
        merged[1, low, :] = (
            ref[rows((me + 3) % 4 * size + cut, size - cut), :].astype(F32)
            + land[1, low, :].astype(F32)
        ).astype(BF)
        out.append(send(merged.at[1, low], land.at[5, low], left))
        return copies + out

    def ring_end(ref, land, axis, size, cut, copies):
        me = axes[axis][0]
        top, low = pl.ds(0, cut), pl.ds(0, size - cut)
        arrived(copies[2:])
        a = ref[rows(me * size, cut), :].astype(F32)
        a = a + land[3, top, :].astype(F32) + land[4, top, :].astype(F32)
        b = ref[rows(me * size + cut, size - cut), :].astype(F32)
        b = b + land[2, low, :].astype(F32) + land[5, low, :].astype(F32)
        return a.astype(BF), b.astype(BF)

    def sum_start(g):
        return [
            ring_start(ref.at[g], s1.at[g, half], half, 288, 144)
            for half, ref in enumerate((g1, g2))
        ]

    def sum_middle(g, copies):
        return [
            ring_middle(ref.at[g], s1.at[g, half], m1.at[g, half], half, 288, 144, copies[half])
            for half, ref in enumerate((g1, g2))
        ]

    def second_start(g, copies):
        out = []
        for half, (ref, spread) in enumerate(((g1, first), (g2, second))):
            a, b = ring_end(ref.at[g], s1.at[g, half], half, 288, 144, copies[half])
            q1[g, half] = (mm(spread[:, 0:144], a) + mm(spread[:, 144:288], b)).astype(BF)
            out.append(ring_start(q1.at[g, half], s2.at[g, half], 1 - half, 80, 48))
        return out

    def second_middle(g, copies):
        return [
            ring_middle(
                q1.at[g, half], s2.at[g, half], m2.at[g, half], 1 - half, 80, 48, copies[half]
            )
            for half in range(2)
        ]

    def z_start(g, copies):
        total = 0.0
        for half, spread in enumerate((upper, lower)):
            a, b = ring_end(q1.at[g, half], s2.at[g, half], 1 - half, 80, 48, copies[half])
            total = total + mm(spread[:, 0:48], a) + mm(spread[:, 48:80], b)
        zb[g] = total.astype(BF)
        if g == 0:
            return [
                send(zb.at[0, rows((z + dz) % 4 * 48, 48)], zr.at[dz - 1], z_same[dz - 1])
                for dz in (1, 2, 3)
            ]
        return [
            send(zb.at[1, rows((z + dz) % 4 * 48, 48)], zr.at[3 + dz], z_other[dz])
            for dz in range(4)
        ]

    mod_t[...] = mod[...].T
    both_t[:, 0:256] = mm(turn[...], mod_t[...]).astype(BF)
    forward(own)
    arrived(grd2)
    to_core(1).wait_recv()
    gs[...] = (full[1].astype(F32) * gate).astype(BF)
    both_t[:, 256:512] = mm(turn[...], gs[...].T).astype(BF)
    cotangent(own)
    attention()
    made = grads(0)
    sum_a = sum_start(0)
    shares(0, own, made)
    arrived(w_last)
    forward(other)
    cotangent(other)
    sum_a = sum_middle(0, sum_a)
    attention()
    made = grads(1)
    sum_b = sum_start(1)
    sum_a = second_start(0, sum_a)
    shares(1, other, made)

    cs[0] = ao[128:256, :].astype(BF)
    cs[1] = gm[128:256, :].astype(BF)
    swapped = [send(cs.at[i], cr.at[i], core) for i in range(2)]
    sum_b = sum_middle(1, sum_b)
    sum_a = second_middle(0, sum_a)

    def back_stage2(which):
        block = rows((x * 2 + yl) * 16, 16)
        back[which, block, :] = ob[which, 0:16, :]
        return [
            send(ob.at[which, pl.ds(slot * 16, 16)], back.at[which, block], stage2_from[slot])
            for slot in range(1, 8)
        ]

    def back_stage1(which):
        backp[which] = mm(swap[...], back[which]).astype(BF)
        block = rows((z * 2 + yh) * 16, 16)
        fin[which, block, :] = backp[which, 0:16, :]
        return [
            send(backp.at[which, pl.ds(slot * 16, 16)], fin.at[which, block], stage1_from[slot])
            for slot in range(1, 8)
        ]

    swapped[0].wait_recv()
    ob[0] = (
        full[0, 0:128, :].astype(F32) + gate * (ao[0:128, :] + cr[0].astype(F32))
    ).astype(BF)
    res2 = back_stage2(0)
    swapped[1].wait_recv()

    def layer_back(i, carry):
        at = pl.ds(pl.multiple_of(i * 32, 32), 32)
        field = full[0, at, :].astype(F32)
        mean = jnp.mean(field, axis=-1, keepdims=True)
        centred = field - mean
        spread = jnp.mean(centred * centred, axis=-1, keepdims=True)
        r = lax.rsqrt(spread + 1e-06)
        hat = centred * r
        d = (gm[at, :] + cr[1, at, :].astype(F32)) * (1.0 + scale)
        dx = r * (
            d
            - jnp.mean(d, axis=-1, keepdims=True)
            - hat * jnp.mean(d * hat, axis=-1, keepdims=True)
        )
        ob[1, at, :] = (full[1, at, :].astype(F32) + dx).astype(BF)
        return carry

    lax.fori_loop(0, 4, layer_back, 0)
    gin2 = back_stage2(1)
    sum_a = z_start(0, sum_a)
    arrived(res2)
    res1 = back_stage1(0)
    sum_b = second_start(1, sum_b)
    arrived(gin2)
    gin1 = back_stage1(1)
    sum_b = second_middle(1, sum_b)
    sum_b = z_start(1, sum_b)
    arrived(res1)
    res_out[...] = fin[0]
    arrived(gin1)
    gin_out[...] = fin[1]
    arrived(sum_a)
    arrived(sum_b)
    total = zb[0, rows(z * 48, 48), :].astype(F32)
    for i in range(7):
        total = total + zr[i].astype(F32)
    inproj_out[:, 0, :] = total[0:18, 0:HC]
    inproj_out[:, 1, :] = total[18:36, 0:HC]
    inproj_out[:, 2, :] = total[0:18, HC : 2 * HC]
    outproj_out[...] = total[18:36, HC : 2 * HC]
    for copy in started:
        copy.wait_send()


N_COPY = 160


def body(tokens_in, mod_shift, mod_scale, branch_gate, inproj, outproj, norm_gain, grad_result):
    swap, turn, first, second, upper, lower, heads = constants()
    vm = pl.BlockSpec(memory_space=pltpu.VMEM)
    anys = pl.BlockSpec(memory_space=pl.ANY)

    def vmem(shape, dtype=BF):
        return pltpu.VMEM(shape, dtype)

    result, grad_in, grad_inproj, grad_outproj = pl.pallas_call(
        kernel,
        out_shape=(
            jax.ShapeDtypeStruct((128, D), BF),
            jax.ShapeDtypeStruct((128, D), BF),
            jax.ShapeDtypeStruct((18, 3, HC), F32),
            jax.ShapeDtypeStruct((18, HC), F32),
        ),
        in_specs=[vm] * 6 + [anys] * 2 + [vm, anys] + [vm] * 5,
        out_specs=(vm, vm, vm, vm),
        scratch_shapes=[
            vmem((D, D)),
            vmem((D, D)),
            vmem((2, D, W2)),
            vmem((2, 128, D)),
            vmem((2, 128, D)),
            vmem((2, 256, D)),
            vmem((256, D)),
            vmem((D, 256)),
            vmem((D, 512)),
            vmem((256, D)),
            vmem((256, HC), F32),
            vmem((256, HC), F32),
            vmem((256, HC)),
            vmem((256, HC)),
            vmem((256, HC)),
            vmem((256, HC)),
            vmem((256, HC), F32),
            vmem((256, HC), F32),
            vmem((256, HC), F32),
            vmem((256, HC), F32),
            vmem((256, HC), F32),
            vmem((256, HC), F32),
            vmem((256, D), F32),
            vmem((256, D), F32),
            vmem((256, W2)),
            vmem((512, W2)),
            vmem((2, D, W2)),
            vmem((2, D, W2)),
            vmem((2, 2, 2, 144, W2)),
            vmem((2, 2, 6, 144, W2)),
            vmem((2, 2, 320, W2)),
            vmem((2, 2, 2, 48, W2)),
            vmem((2, 2, 6, 48, W2)),
            vmem((2, 192, W2)),
            vmem((7, 48, W2)),
            vmem((2, 128, D)),
            vmem((2, 128, D)),
            vmem((2, 128, D)),
            vmem((2, 128, D)),
            vmem((2, 128, D)),
            vmem((2, 128, D)),
            pltpu.SemaphoreType.DMA((3,)),
            pltpu.SemaphoreType.DMA((N_COPY,)),
            pltpu.SemaphoreType.DMA((N_COPY,)),
        ],
        compiler_params=pltpu.CompilerParams(
            collective_id=0, has_side_effects=True, vmem_limit_bytes=58 * 2**20
        ),
        name="sublayer",
    )(
        tokens_in, grad_result, mod_shift, mod_scale, branch_gate, norm_gain,
        jnp.transpose(inproj, (1, 2, 0)).reshape(3 * HC, D), outproj,
        swap, turn, first, second, upper, lower, heads,
    )
    return result, grad_in, grad_inproj, grad_outproj.T


def solution(mesh):
    placed = (
        P(("frame", "head"), None),
        P(),
        P(),
        P(),
        P(None, None, "head"),
        P("head", None),
        P(),
        P(("frame", "head"), None),
    )
    return jax.shard_map(
        body,
        mesh=mesh,
        in_specs=placed,
        out_specs=(
            P(("frame", "head"), None),
            P(("frame", "head"), None),
            P("frame", None, "head"),
            P("head", "frame"),
        ),
        check_vma=False,
    )
```

```python
import functools

import jax
import jax.numpy as jnp
import ml_dtypes
import numpy as np
from jax import lax
from jax.experimental import pallas as pl
from jax.experimental.pallas import tpu as pltpu
from jax.sharding import PartitionSpec as P

D = 1152
HD = 72
W2 = 640
W1 = D - W2
HC = 288
BF = jnp.bfloat16
F32 = jnp.float32
MESH = pl.DeviceIdType.MESH

def one_hot(rows, cols, source):
    made = np.zeros((rows, cols), np.float32)
    for row in range(rows):
        col = source(row)
        if col is not None:
            made[row, col] = 1.0
    return made.astype(ml_dtypes.bfloat16)


def constants():
    swap = one_hot(128, 128, lambda o: (o // 2 % 8) * 16 + (o // 16) * 2 + o % 2)
    turn = one_hot(
        D, D, lambda t: (t % 288 // 72) * 288 + (t % 72 // 18) * 72 + (t // 288) * 18 + t % 18
    )
    first = one_hot(
        320,
        288,
        lambda o: (o % 80 // 18) * 72 + (o // 80) * 18 + o % 80 % 18 if o % 80 < 72 else None,
    )
    second = one_hot(320, 288, lambda o: (o // 80) * 72 + o % 80 if o % 80 < 72 else None)
    upper = one_hot(192, 80, lambda o: (o // 48) * 18 + o % 48 if o % 48 < 18 else None)
    lower = one_hot(
        192, 80, lambda o: (o // 48) * 18 + o % 48 - 18 if 18 <= o % 48 < 36 else None
    )
    heads = np.zeros((HC, HC), np.float32)
    for h in range(4):
        heads[h * HD : (h + 1) * HD, h * HD : (h + 1) * HD] = 1.0
    return (swap, turn, first, second, upper, lower, heads.astype(ml_dtypes.bfloat16))


def mm(a, b):
    return jnp.dot(a, b, preferred_element_type=F32)


def mm_nt(a, b):
    return lax.dot_general(a, b, (((1,), (1,)), ((), ())), preferred_element_type=F32)


def mm_tn(a, b):
    return lax.dot_general(a, b, (((0,), (0,)), ((), ())), preferred_element_type=F32)


def head_sum(values, ones):
    high = values.astype(BF)
    low = (values - high.astype(F32)).astype(BF)
    return mm(high, ones) + mm(low, ones)


def kernel(
    tok, grd, shift_in, scale_in, gate_in, gain_in, swap, heads, w_in, w_out, turn_hbm,
    first_hbm, second_hbm, upper_hbm, lower_hbm,
    res_out, gin_out, inproj_out, outproj_out,
    wown, turn, first, second, upper, lower, wo, ta1, ta2, ga1, ga2, ga3, ga4, full, mod, mod_t, both_t, gs, qf, kf, qn, kn, vn, ga, rq, rk,
    acc_o, acc_q, acc_k, acc_v, ao, gm, gx1, gx2, g1, g2, m1, s1, q1, s2, zb, zr, cs, cr,
    ob, back, backp, fin,
    local_sem, ssem, rsem,
):
    f = lax.axis_index("frame")
    h = lax.axis_index("head")
    x, z, yh, yl = f // 16, (f // 4) % 4, (f // 2) % 2, f % 2
    zh, c = h // 2, h % 2
    y = yh * 2 + yl

    def dev(px=x, pz=z, py=y, ph=zh, pc=c):
        return ((px * 4 + pz) * 4 + py, ph * 2 + pc)

    def flip(dh, dl):
        return ((yh + dh) % 2) * 2 + (yl + dl) % 2

    stage1_to = [dev(pz=(z + dz) % 4, py=flip(dh, 0)) for dz in range(4) for dh in range(2)]
    stage1_at = [((z + dz) % 4) * 2 + (yh + dh) % 2 for dz in range(4) for dh in range(2)]
    stage1_from = [dev(pz=(z - dz) % 4, py=flip(dh, 0)) for dz in range(4) for dh in range(2)]
    stage2_to = [dev(px=(x + dx) % 4, py=flip(0, dl)) for dx in range(4) for dl in range(2)]
    stage2_at = [((x + dx) % 4) * 2 + (yl + dl) % 2 for dx in range(4) for dl in range(2)]
    stage2_from = [dev(px=(x - dx) % 4, py=flip(0, dl)) for dx in range(4) for dl in range(2)]
    core = dev(pc=1 - c)
    mirror = dev(pz=3 - z, ph=1 - zh)
    z_other = [dev(pz=(z + dz) % 4, ph=1 - zh) for dz in range(4)]
    z_same = [dev(pz=(z + dz) % 4) for dz in (1, 2, 3)]
    partners = stage1_to[1:] + stage2_to[1:] + [dev(py=flip(1, 1)), core] + z_other

    count = [0]
    started = []

    def send(src, dst, to):
        at = count[0]
        count[0] += 1
        copy = pltpu.make_async_remote_copy(
            src_ref=src, dst_ref=dst, send_sem=ssem.at[at], recv_sem=rsem.at[at],
            device_id=to, device_id_type=MESH,
        )
        copy.start()
        started.append(copy)
        return copy

    def rows(start, size):
        return pl.ds(pl.multiple_of(start, 16), size)

    def arrived(copies):
        for copy in copies:
            copy.wait_recv()

    loads = [
        pltpu.make_async_copy(src, dst, local_sem.at[i])
        for i, (src, dst) in enumerate(
            (
                (w_in, wown.at[pl.ds(0, 864)]),
                (w_out, wown.at[pl.ds(864, HC)]),
                (turn_hbm, turn),
                (first_hbm, first),
                (second_hbm, second),
                (upper_hbm, upper),
                (lower_hbm, lower),
            )
        )
    ]
    for load in loads:
        load.start()

    barrier = pltpu.get_barrier_semaphore()
    for to in partners:
        pl.semaphore_signal(barrier, inc=1, device_id=to, device_id_type=MESH)
    ga1[...] = mm(swap[...], grd[...]).astype(BF)
    loads[0].wait()
    loads[1].wait()
    pl.semaphore_wait(barrier, len(partners))

    def spread(src, dst, places, targets):
        out = []
        for slot in range(8):
            block = rows(places[slot] * 16, 16)
            if slot == 0:
                dst[0:16, :] = src[block, :]
            else:
                out.append(send(src.at[block], dst.at[pl.ds(slot * 16, 16)], targets[slot]))
        return out

    def to_core(which):
        return send(full.at[which, pl.ds(0, 128)], full.at[which, pl.ds(128, 128)], core)

    def piece(px, py):
        return py % 2, (px * 2 + py // 2) * 144

    part, start = piece(x, y)
    lanes = pl.ds(pl.multiple_of(part * 512, 128), W2)
    w_z = [
        send(wown.at[rows(start + at, size), lanes], wo.at[part, rows(start + at, size)], mirror)
        for at, size in ((0, 80), (80, 64))
    ]
    tok1 = spread(tok, ta1, stage1_at, stage1_to)
    grd1 = spread(ga1, ga2, stage2_at, stage2_to)

    flips = ((0, 1), (1, 0), (1, 1))

    def over_x(pc, at, size):
        ref = wo.at[pc, rows(at, size)]
        return [send(ref, ref, dev(px=(x + dx) % 4)) for dx in (1, 2, 3)]

    def over_y(pc, at, size):
        ref = wo.at[pc, rows(at, size)]
        return [send(ref, ref, dev(py=flip(*d))) for d in flips]

    arrived(grd1)
    ga3[...] = mm(swap[...], ga2[...]).astype(BF)
    grd2 = spread(ga3, ga4, stage1_at, stage1_to)
    w_z[0].wait_recv()
    w_x1 = over_x(part, start, 80)
    w_z[1].wait_recv()
    w_y1 = over_y(part, start + 80, 64)
    arrived(tok1)
    ta2[...] = mm(swap[...], ta1[...]).astype(BF)
    tok2 = spread(ta2, full.at[0], stage2_at, stage2_to)
    w_last = over_y(part, start, 80) + over_x(part, start + 80, 64)
    for copy, dx in zip(w_x1, (1, 2, 3)):
        copy.wait_recv()
        pc, at = piece((x - dx) % 4, y)
        w_last += over_y(pc, at, 80)
    for copy, d in zip(w_y1, flips):
        copy.wait_recv()
        pc, at = piece(x, flip(*d))
        w_last += over_x(pc, at + 80, 64)
    shift = shift_in[...].reshape(1, D)
    scale = scale_in[...].reshape(1, D)
    gate = gate_in[...].reshape(1, D)

    def modulate(i, carry):
        at = pl.ds(pl.multiple_of(i * 32, 32), 32)
        field = full[0, at, :].astype(F32)
        mean = jnp.mean(field, axis=-1, keepdims=True)
        centred = field - mean
        spread = jnp.mean(centred * centred, axis=-1, keepdims=True)
        mod[at, :] = (centred * lax.rsqrt(spread + 1e-06) * (1.0 + scale) + shift).astype(BF)
        return carry

    arrived(tok2)
    tok3 = to_core(0)
    arrived(grd2)
    full[1, 0:128, :] = mm(swap[...], ga4[...]).astype(BF)
    grd3 = to_core(1)
    lax.fori_loop(0, 4, modulate, 0)
    tok3.wait_recv()
    lax.fori_loop(4, 8, modulate, 0)
    for load in loads[2:]:
        load.wait()

    lane = lax.broadcasted_iota(jnp.int32, (1, HC), 1)
    row_i = lax.broadcasted_iota(jnp.int32, (256, 256), 0)
    col_i = lax.broadcasted_iota(jnp.int32, (256, 256), 1)
    gain_q = jnp.concatenate([gain_in[0:1, :]] * 4, axis=1)
    gain_k = jnp.concatenate([gain_in[1:2, :]] * 4, axis=1)

    def own(j):
        at = pl.ds(j * HC, HC)
        return wown[at, 0:W2], wown[at, W2:D]

    def other(j):
        at = pl.ds(j * HC, HC)
        return wo[0, at, :], wo[1, at, W2 - W1 : W2]

    def project(act, w, j):
        low, high = w(j)
        return mm_nt(act[:, 0:W2], low) + mm_nt(act[:, W2:D], high)

    def forward(w):
        q = project(mod, w, 0)
        qf[...] = q
        r = lax.rsqrt(head_sum(q * q, heads[...]) * (1.0 / HD) + 1e-06)
        rq[...] = r
        qn[...] = (q * r * gain_q).astype(BF)
        k = project(mod, w, 1)
        kf[...] = k
        r = lax.rsqrt(head_sum(k * k, heads[...]) * (1.0 / HD) + 1e-06)
        rk[...] = r
        kn[...] = (k * r * gain_k).astype(BF)
        vn[...] = project(mod, w, 2).astype(BF)

    def cotangent(w):
        ga[...] = project(gs, w, 3).astype(BF)

    def attention():
        acc_o[...] = jnp.zeros_like(acc_o)
        acc_q[...] = jnp.zeros_like(acc_q)
        acc_k[...] = jnp.zeros_like(acc_k)
        acc_v[...] = jnp.zeros_like(acc_v)
        same = (row_i // 128 == col_i // 128) & (row_i % 2 == col_i % 2)
        root = 1.0 / np.sqrt(np.float32(HD))

        def head(i, carry):
            inside = (lane >= i * HD) & (lane < i * HD + HD)
            zero = jnp.zeros((), BF)
            qh = jnp.where(inside, qn[...], zero)
            kh = jnp.where(inside, kn[...], zero)
            vh = jnp.where(inside, vn[...], zero)
            gh = jnp.where(inside, ga[...], zero)
            s = jnp.where(same, mm_nt(qh, kh) * root, -1e30)
            e = jnp.exp(s - jnp.max(s, axis=-1, keepdims=True))
            p = e * (1.0 / jnp.sum(e, axis=-1, keepdims=True))
            pb = p.astype(BF)
            acc_o[...] += mm(pb, vh)
            acc_v[...] += mm_tn(pb, gh)
            dp = mm_nt(gh, vh)
            ds = (p * (dp - jnp.sum(p * dp, axis=-1, keepdims=True)) * root).astype(BF)
            acc_q[...] += mm(ds, kh)
            acc_k[...] += mm_tn(ds, qh)
            return carry

        lax.fori_loop(0, 4, head, 0, unroll=2)

    def unnorm(cot, raw, r, gain):
        n = raw * r
        dn = cot.astype(BF).astype(F32) * gain
        inner = head_sum(n * dn, heads[...]) * (1.0 / HD)
        return (r * (dn - n * inner)).astype(BF)

    axes = (
        (x, dev(px=(x + 1) % 4), dev(px=(x - 1) % 4)),
        (y, dev(py=(y + 1) % 4), dev(py=(y - 1) % 4)),
    )

    def ring_send(ref, land, axis, k, copies):
        me, right, left = axes[axis]
        start = (me + k) % 4 * 288
        top, low = ref.at[rows(start, 144)], ref.at[rows(start + 144, 144)]
        if k == 2:
            copies[0] = send(top, land.at[0], right)
            copies[1] = send(low, land.at[1], left)
        elif k == 1:
            copies[2] = send(low, land.at[2], right)
        elif k == 3:
            copies[3] = send(top, land.at[3], left)

    def ring_middle(ref, land, merged, axis, copies):
        me, right, left = axes[axis]
        for i, (at, to) in enumerate((((me + 1) % 4 * 288, right), ((me + 3) % 4 * 288 + 144, left))):
            copies[i].wait_recv()
            merged[i] = (ref[rows(at, 144), :].astype(F32) + land[i].astype(F32)).astype(BF)
            copies.append(send(merged.at[i], land.at[4 + i], to))

    def ring_end(ref, land, axis, copies):
        me = axes[axis][0]
        arrived(copies[2:])
        a = ref[rows(me * 288, 144), :].astype(F32)
        a = a + land[3].astype(F32) + land[4].astype(F32)
        b = ref[rows(me * 288 + 144, 144), :].astype(F32)
        b = b + land[2].astype(F32) + land[5].astype(F32)
        return a.astype(BF), b.astype(BF)

    def sum_middle(g, copies):
        for half, ref in enumerate((g1, g2)):
            ring_middle(ref.at[g], s1.at[g, half], m1.at[g, half], half, copies[half])

    def second_start(g, copies):
        out = []
        for half, (ref, spread) in enumerate(((g1, first), (g2, second))):
            a, b = ring_end(ref.at[g], s1.at[g, half], half, copies[half])
            q1[g, half] = (mm(spread[:, 0:144], a) + mm(spread[:, 144:288], b)).astype(BF)
            if half == 0:
                to = [(flip(*d), dev(py=flip(*d))) for d in flips]
            else:
                to = [((x + dx) % 4, dev(px=(x + dx) % 4)) for dx in (1, 2, 3)]
            out += [
                send(q1.at[g, half, rows(at * 80, 80)], s2.at[g, half, i], target)
                for i, (at, target) in enumerate(to)
            ]
        return out

    def z_start(g, copies):
        arrived(copies)
        total = 0.0
        for half, (spread, me) in enumerate(((upper, y), (lower, x))):
            part = q1[g, half, rows(me * 80, 80), :].astype(F32)
            for i in range(3):
                part = part + s2[g, half, i].astype(F32)
            total = total + mm(spread[...], part.astype(BF))
        zb[g] = total.astype(BF)
        if g == 0:
            return [
                send(zb.at[0, rows((z + dz) % 4 * 48, 48)], zr.at[dz - 1], z_same[dz - 1])
                for dz in (1, 2, 3)
            ]
        return [
            send(zb.at[1, rows((z + dz) % 4 * 48, 48)], zr.at[3 + dz], z_other[dz])
            for dz in range(4)
        ]

    def grads(g):
        gq = unnorm(acc_q[...], qf[...], rq[...], gain_q)
        gk = unnorm(acc_k[...], kf[...], rk[...], gain_k)
        gv = acc_v[...].astype(BF)
        att = acc_o[...].astype(BF)
        pad = jnp.zeros((256, W2 - 2 * HC), BF)
        gx1[...] = jnp.concatenate([gq, gv, pad], axis=1)
        gx2[0:256, :] = jnp.concatenate([gk, jnp.zeros((256, W2 - HC), BF)], axis=1)
        gx2[256:512, :] = jnp.concatenate([jnp.zeros((256, HC), BF), att, pad], axis=1)

        copies = [[None] * 4, [None] * 4]
        for k in (2, 1, 3, 0):
            for half, (ref, left, right) in enumerate(((g1, mod_t, gx1), (g2, both_t, gx2))):
                at = rows((axes[half][0] + k) % 4 * 288, 288)
                ref[g, at, :] = mm(left[at, :], right[...]).astype(BF)
                ring_send(ref.at[g], s1.at[g, half], half, k, copies[half])
        return copies, (gq, gk, gv, att)


    def shares(g, w, parts):
        gq, gk, gv, att = parts
        (q0, q1_), (k0, k1_), (v0, v1_), (o0, o1_) = w(0), w(1), w(2), w(3)
        pieces = (
            (ao, pl.ds(0, W2), mm(att, o0)),
            (ao, pl.ds(W2, W1), mm(att, o1_)),
            (gm, pl.ds(0, W2), mm(gq, q0) + mm(gk, k0) + mm(gv, v0)),
            (gm, pl.ds(W2, W1), mm(gq, q1_) + mm(gk, k1_) + mm(gv, v1_)),
        )
        for ref, at, value in pieces:
            if g == 0:
                ref[:, at] = value
            else:
                ref[:, at] += value

    mod_t[...] = mod[...].T
    both_t[:, 0:256] = mm(turn[...], mod_t[...]).astype(BF)
    forward(own)
    grd3.wait_recv()
    gs[...] = (full[1].astype(F32) * gate).astype(BF)
    both_t[:, 256:512] = mm(turn[...], gs[...].T).astype(BF)
    cotangent(own)
    attention()
    sum_a, made = grads(0)
    shares(0, own, made)
    arrived(w_last)
    forward(other)
    cotangent(other)
    sum_middle(0, sum_a)
    attention()
    sum_b, made = grads(1)
    shares(1, other, made)

    cs[0] = ao[128:256, :].astype(BF)
    cs[1] = gm[128:256, :].astype(BF)
    swapped = [send(cs.at[i], cr.at[i], core) for i in range(2)]
    sum_a = second_start(0, sum_a)

    def back_first(which):
        ob[which] = mm(swap[...], ob[which]).astype(BF)
        block = rows((z * 2 + yh) * 16, 16)
        back[which, block, :] = ob[which, 0:16, :]
        return [
            send(ob.at[which, pl.ds(slot * 16, 16)], back.at[which, block], stage1_from[slot])
            for slot in range(1, 8)
        ]

    def back_last(which):
        backp[which] = mm(swap[...], back[which]).astype(BF)
        block = rows((x * 2 + yl) * 16, 16)
        fin[which, block, :] = backp[which, 0:16, :]
        return [
            send(backp.at[which, pl.ds(slot * 16, 16)], fin.at[which, block], stage2_from[slot])
            for slot in range(1, 8)
        ]

    swapped[0].wait_recv()
    ob[0] = (
        full[0, 0:128, :].astype(F32) + gate * (ao[0:128, :] + cr[0].astype(F32))
    ).astype(BF)
    res_z = back_first(0)
    sum_middle(1, sum_b)
    swapped[1].wait_recv()

    def layer_back(i, carry):
        at = pl.ds(pl.multiple_of(i * 32, 32), 32)
        field = full[0, at, :].astype(F32)
        mean = jnp.mean(field, axis=-1, keepdims=True)
        centred = field - mean
        spread = jnp.mean(centred * centred, axis=-1, keepdims=True)
        r = lax.rsqrt(spread + 1e-06)
        hat = centred * r
        d = (gm[at, :] + cr[1, at, :].astype(F32)) * (1.0 + scale)
        dx = r * (
            d
            - jnp.mean(d, axis=-1, keepdims=True)
            - hat * jnp.mean(d * hat, axis=-1, keepdims=True)
        )
        ob[1, at, :] = (full[1, at, :].astype(F32) + dx).astype(BF)
        return carry

    lax.fori_loop(0, 4, layer_back, 0)
    gin_z = back_first(1)
    sum_a = z_start(0, sum_a)
    sum_b = second_start(1, sum_b)
    arrived(res_z)
    res_xy = back_last(0)
    arrived(gin_z)
    gin_xy = back_last(1)
    sum_b = z_start(1, sum_b)
    arrived(res_xy)
    res_out[...] = mm(swap[...], fin[0]).astype(BF)
    arrived(gin_xy)
    gin_out[...] = mm(swap[...], fin[1]).astype(BF)
    arrived(sum_a)
    arrived(sum_b)
    total = zb[0, rows(z * 48, 48), :].astype(F32)
    for i in range(7):
        total = total + zr[i].astype(F32)
    inproj_out[:, 0, :] = total[0:18, 0:HC]
    inproj_out[:, 1, :] = total[18:36, 0:HC]
    inproj_out[:, 2, :] = total[0:18, HC : 2 * HC]
    outproj_out[...] = total[18:36, HC : 2 * HC]
    for copy in started:
        copy.wait_send()


def place(*refs):
    for i in range(4):
        refs[4 + i][...] = refs[i][...]


N_COPY = 160


def body(tokens_in, mod_shift, mod_scale, branch_gate, inproj, outproj, norm_gain, grad_result):
    swap, turn, first, second, upper, lower, heads = constants()
    vm = pl.BlockSpec(memory_space=pltpu.VMEM)
    anys = pl.BlockSpec(memory_space=pl.ANY)

    def vmem(shape, dtype=BF):
        return pltpu.VMEM(shape, dtype)

    result, grad_in, grad_inproj, grad_outproj = pl.pallas_call(
        kernel,
        out_shape=(
            jax.ShapeDtypeStruct((128, D), BF),
            jax.ShapeDtypeStruct((128, D), BF),
            jax.ShapeDtypeStruct((18, 3, HC), F32),
            jax.ShapeDtypeStruct((18, HC), F32),
        ),
        in_specs=[vm] * 8 + [anys] * 7,
        out_specs=(vm, vm, vm, vm),
        scratch_shapes=[
            vmem((D, D)),
            vmem((D, D)),
            vmem((320, 288)),
            vmem((320, 288)),
            vmem((192, 80)),
            vmem((192, 80)),
            vmem((2, D, W2)),
            *[vmem((128, D))] * 6,
            vmem((2, 256, D)),
            vmem((256, D)),
            vmem((D, 256)),
            vmem((D, 512)),
            vmem((256, D)),
            vmem((256, HC), F32),
            vmem((256, HC), F32),
            vmem((256, HC)),
            vmem((256, HC)),
            vmem((256, HC)),
            vmem((256, HC)),
            vmem((256, HC), F32),
            vmem((256, HC), F32),
            vmem((256, HC), F32),
            vmem((256, HC), F32),
            vmem((256, HC), F32),
            vmem((256, HC), F32),
            vmem((256, D), F32),
            vmem((256, D), F32),
            vmem((256, W2)),
            vmem((512, W2)),
            vmem((2, D, W2)),
            vmem((2, D, W2)),
            vmem((2, 2, 2, 144, W2)),
            vmem((2, 2, 6, 144, W2)),
            vmem((2, 2, 320, W2)),
            vmem((2, 2, 3, 80, W2)),
            vmem((2, 192, W2)),
            vmem((7, 48, W2)),
            vmem((2, 128, D)),
            vmem((2, 128, D)),
            vmem((2, 128, D)),
            vmem((2, 128, D)),
            vmem((2, 128, D)),
            vmem((2, 128, D)),
            pltpu.SemaphoreType.DMA((7,)),
            pltpu.SemaphoreType.DMA((N_COPY,)),
            pltpu.SemaphoreType.DMA((N_COPY,)),
        ],
        compiler_params=pltpu.CompilerParams(
            collective_id=0, has_side_effects=True, vmem_limit_bytes=58 * 2**20
        ),
        name="sublayer",
    )(
        tokens_in, grad_result, mod_shift, mod_scale, branch_gate, norm_gain, swap, heads,
        jnp.transpose(inproj, (1, 2, 0)).reshape(3 * HC, D), outproj,
        turn, first, second, upper, lower,
    )
    made = [result, grad_in, grad_inproj, grad_outproj]
    result, grad_in, grad_inproj, grad_outproj = pl.pallas_call(
        place,
        out_shape=[jax.ShapeDtypeStruct(v.shape, v.dtype) for v in made],
        in_specs=[vm] * 4,
        out_specs=[vm] * 4,
        name="place",
    )(*made)
    return result, grad_in, grad_inproj, grad_outproj.T


def solution(mesh):
    placed = (
        P(("frame", "head"), None),
        P(),
        P(),
        P(),
        P(None, None, "head"),
        P("head", None),
        P(),
        P(("frame", "head"), None),
    )
    return jax.shard_map(
        body,
        mesh=mesh,
        in_specs=placed,
        out_specs=(
            P(("frame", "head"), None),
            P(("frame", "head"), None),
            P("frame", None, "head"),
            P("head", "frame"),
        ),
        check_vma=False,
    )
```

```python
import functools

import jax
import jax.numpy as jnp
import ml_dtypes
import numpy as np
from jax import lax
from jax.experimental import pallas as pl
from jax.experimental.pallas import tpu as pltpu
from jax.sharding import PartitionSpec as P

D = 1152
HD = 72
W2 = 640
W1 = D - W2
HC = 288
BF = jnp.bfloat16
F32 = jnp.float32
MESH = pl.DeviceIdType.MESH

def one_hot(rows, cols, source):
    made = np.zeros((rows, cols), np.float32)
    for row in range(rows):
        col = source(row)
        if col is not None:
            made[row, col] = 1.0
    return made.astype(ml_dtypes.bfloat16)


def constants():
    swap = one_hot(128, 128, lambda o: (o // 2 % 8) * 16 + (o // 16) * 2 + o % 2)
    turn = one_hot(
        D, D, lambda t: (t % 288 // 72) * 288 + (t % 72 // 18) * 72 + (t // 288) * 18 + t % 18
    )
    first = one_hot(
        320,
        288,
        lambda o: (o % 80 // 18) * 72 + (o // 80) * 18 + o % 80 % 18 if o % 80 < 72 else None,
    )
    second = one_hot(320, 288, lambda o: (o // 80) * 72 + o % 80 if o % 80 < 72 else None)
    upper = one_hot(192, 80, lambda o: (o // 48) * 18 + o % 48 if o % 48 < 18 else None)
    lower = one_hot(
        192, 80, lambda o: (o // 48) * 18 + o % 48 - 18 if 18 <= o % 48 < 36 else None
    )
    heads = np.zeros((HC, HC), np.float32)
    for h in range(4):
        heads[h * HD : (h + 1) * HD, h * HD : (h + 1) * HD] = 1.0
    return (swap, turn, first, second, upper, lower, heads.astype(ml_dtypes.bfloat16))


def mm(a, b):
    return jnp.dot(a, b, preferred_element_type=F32)


def mm_nt(a, b):
    return lax.dot_general(a, b, (((1,), (1,)), ((), ())), preferred_element_type=F32)


def mm_tn(a, b):
    return lax.dot_general(a, b, (((0,), (0,)), ((), ())), preferred_element_type=F32)


def head_sum(values, ones):
    high = values.astype(BF)
    low = (values - high.astype(F32)).astype(BF)
    return mm(high, ones) + mm(low, ones)


def kernel(
    tok, grd, shift_in, scale_in, gate_in, gain_in, swap, heads, w_in, w_out, turn_hbm,
    first_hbm, second_hbm, upper_hbm, lower_hbm,
    res_out, gin_out, inproj_out, outproj_out,
    wown, turn, first, second, upper, lower, wo, ta1, ta2, ga1, ga2, ga3, ga4, full, mod, mod_t, both_t, gs, qf, kf, qn, kn, vn, ga, rq, rk,
    acc_o, acc_q, acc_k, acc_v, ao, gm, gx1, gx2, g1, g2, m1, s1, q1, s2, zb, zr, cs, cr,
    ob, back, backp, fin,
    local_sem, ssem, rsem,
):
    f = lax.axis_index("frame")
    h = lax.axis_index("head")
    x, z, yh, yl = f // 16, (f // 4) % 4, (f // 2) % 2, f % 2
    zh, c = h // 2, h % 2
    y = yh * 2 + yl

    def dev(px=x, pz=z, py=y, ph=zh, pc=c):
        return ((px * 4 + pz) * 4 + py, ph * 2 + pc)

    def flip(dh, dl):
        return ((yh + dh) % 2) * 2 + (yl + dl) % 2

    stage1_to = [dev(pz=(z + dz) % 4, py=flip(dh, 0)) for dz in range(4) for dh in range(2)]
    stage1_at = [((z + dz) % 4) * 2 + (yh + dh) % 2 for dz in range(4) for dh in range(2)]
    stage1_from = [dev(pz=(z - dz) % 4, py=flip(dh, 0)) for dz in range(4) for dh in range(2)]
    stage2_to = [dev(px=(x + dx) % 4, py=flip(0, dl)) for dx in range(4) for dl in range(2)]
    stage2_at = [((x + dx) % 4) * 2 + (yl + dl) % 2 for dx in range(4) for dl in range(2)]
    stage2_from = [dev(px=(x - dx) % 4, py=flip(0, dl)) for dx in range(4) for dl in range(2)]
    core = dev(pc=1 - c)
    mirror = dev(pz=3 - z, ph=1 - zh)
    z_other = [dev(pz=(z + dz) % 4, ph=1 - zh) for dz in range(4)]
    z_same = [dev(pz=(z + dz) % 4) for dz in (1, 2, 3)]
    partners = stage1_to[1:] + stage2_to[1:] + [dev(py=flip(1, 1)), core] + z_other

    count = [0]
    started = []

    def send(src, dst, to):
        at = count[0]
        count[0] += 1
        copy = pltpu.make_async_remote_copy(
            src_ref=src, dst_ref=dst, send_sem=ssem.at[at], recv_sem=rsem.at[at],
            device_id=to, device_id_type=MESH,
        )
        copy.start()
        started.append(copy)
        return copy

    def rows(start, size):
        return pl.ds(pl.multiple_of(start, 16), size)

    def arrived(copies):
        for copy in copies:
            copy.wait_recv()

    loads = [
        pltpu.make_async_copy(src, dst, local_sem.at[i])
        for i, (src, dst) in enumerate(
            (
                (w_in, wown.at[pl.ds(0, 864)]),
                (w_out, wown.at[pl.ds(864, HC)]),
                (turn_hbm, turn),
                (first_hbm, first),
                (second_hbm, second),
                (upper_hbm, upper),
                (lower_hbm, lower),
            )
        )
    ]
    for load in loads:
        load.start()

    barrier = pltpu.get_barrier_semaphore()
    for to in partners:
        pl.semaphore_signal(barrier, inc=1, device_id=to, device_id_type=MESH)
    ga1[...] = mm(swap[...], grd[...]).astype(BF)
    loads[0].wait()
    loads[1].wait()
    pl.semaphore_wait(barrier, len(partners))

    def spread(src, dst, places, targets):
        out = []
        for slot in range(8):
            block = rows(places[slot] * 16, 16)
            if slot == 0:
                dst[0:16, :] = src[block, :]
            else:
                out.append(send(src.at[block], dst.at[pl.ds(slot * 16, 16)], targets[slot]))
        return out

    def to_core(which):
        return send(full.at[which, pl.ds(0, 128)], full.at[which, pl.ds(128, 128)], core)

    def piece(px, py):
        return py % 2, (px * 2 + py // 2) * 144

    part, start = piece(x, y)
    lanes = pl.ds(pl.multiple_of(part * 512, 128), W2)
    w_z = [
        send(wown.at[rows(start + at, size), lanes], wo.at[part, rows(start + at, size)], mirror)
        for at, size in ((0, 80), (80, 64))
    ]
    tok1 = spread(tok, ta1, stage1_at, stage1_to)
    grd1 = spread(ga1, ga2, stage2_at, stage2_to)

    flips = ((0, 1), (1, 0), (1, 1))

    def over_x(pc, at, size):
        ref = wo.at[pc, rows(at, size)]
        return [send(ref, ref, dev(px=(x + dx) % 4)) for dx in (1, 2, 3)]

    def over_y(pc, at, size):
        ref = wo.at[pc, rows(at, size)]
        return [send(ref, ref, dev(py=flip(*d))) for d in flips]

    arrived(grd1)
    ga3[...] = mm(swap[...], ga2[...]).astype(BF)
    grd2 = spread(ga3, ga4, stage1_at, stage1_to)
    w_z[0].wait_recv()
    w_x1 = over_x(part, start, 80)
    w_z[1].wait_recv()
    w_y1 = over_y(part, start + 80, 64)
    arrived(tok1)
    ta2[...] = mm(swap[...], ta1[...]).astype(BF)
    tok2 = spread(ta2, full.at[0], stage2_at, stage2_to)
    w_last = over_y(part, start, 80) + over_x(part, start + 80, 64)
    for copy, dx in zip(w_x1, (1, 2, 3)):
        copy.wait_recv()
        pc, at = piece((x - dx) % 4, y)
        w_last += over_y(pc, at, 80)
    for copy, d in zip(w_y1, flips):
        copy.wait_recv()
        pc, at = piece(x, flip(*d))
        w_last += over_x(pc, at + 80, 64)
    shift = shift_in[...].reshape(1, D)
    scale = scale_in[...].reshape(1, D)
    gate = gate_in[...].reshape(1, D)

    def modulate(i, carry):
        at = pl.ds(pl.multiple_of(i * 32, 32), 32)
        field = full[0, at, :].astype(F32)
        mean = jnp.mean(field, axis=-1, keepdims=True)
        centred = field - mean
        spread = jnp.mean(centred * centred, axis=-1, keepdims=True)
        mod[at, :] = (centred * lax.rsqrt(spread + 1e-06) * (1.0 + scale) + shift).astype(BF)
        return carry

    arrived(tok2)
    tok3 = to_core(0)
    arrived(grd2)
    full[1, 0:128, :] = mm(swap[...], ga4[...]).astype(BF)
    grd3 = to_core(1)
    lax.fori_loop(0, 4, modulate, 0)
    tok3.wait_recv()
    lax.fori_loop(4, 8, modulate, 0)
    for load in loads[2:]:
        load.wait()

    lane = lax.broadcasted_iota(jnp.int32, (1, HC), 1)
    row_i = lax.broadcasted_iota(jnp.int32, (256, 256), 0)
    col_i = lax.broadcasted_iota(jnp.int32, (256, 256), 1)
    gain_q = jnp.concatenate([gain_in[0:1, :]] * 4, axis=1)
    gain_k = jnp.concatenate([gain_in[1:2, :]] * 4, axis=1)

    def own(j):
        at = pl.ds(j * HC, HC)
        return wown[at, 0:W2], wown[at, W2:D]

    def other(j):
        at = pl.ds(j * HC, HC)
        return wo[0, at, :], wo[1, at, W2 - W1 : W2]

    def project(act, w, j):
        low, high = w(j)
        return mm_nt(act[:, 0:W2], low) + mm_nt(act[:, W2:D], high)

    def forward(w):
        q = project(mod, w, 0)
        qf[...] = q
        r = lax.rsqrt(head_sum(q * q, heads[...]) * (1.0 / HD) + 1e-06)
        rq[...] = r
        qn[...] = (q * r * gain_q).astype(BF)
        k = project(mod, w, 1)
        kf[...] = k
        r = lax.rsqrt(head_sum(k * k, heads[...]) * (1.0 / HD) + 1e-06)
        rk[...] = r
        kn[...] = (k * r * gain_k).astype(BF)
        vn[...] = project(mod, w, 2).astype(BF)

    def cotangent(w):
        ga[...] = project(gs, w, 3).astype(BF)

    def attention():
        acc_o[...] = jnp.zeros_like(acc_o)
        acc_q[...] = jnp.zeros_like(acc_q)
        acc_k[...] = jnp.zeros_like(acc_k)
        acc_v[...] = jnp.zeros_like(acc_v)
        same = (row_i // 128 == col_i // 128) & (row_i % 2 == col_i % 2)
        root = 1.0 / np.sqrt(np.float32(HD))

        def head(i, carry):
            inside = (lane >= i * HD) & (lane < i * HD + HD)
            zero = jnp.zeros((), BF)
            qh = jnp.where(inside, qn[...], zero)
            kh = jnp.where(inside, kn[...], zero)
            vh = jnp.where(inside, vn[...], zero)
            gh = jnp.where(inside, ga[...], zero)
            s = jnp.where(same, mm_nt(qh, kh) * root, -1e30)
            e = jnp.exp(s - jnp.max(s, axis=-1, keepdims=True))
            p = e * (1.0 / jnp.sum(e, axis=-1, keepdims=True))
            pb = p.astype(BF)
            acc_o[...] += mm(pb, vh)
            acc_v[...] += mm_tn(pb, gh)
            dp = mm_nt(gh, vh)
            ds = (p * (dp - jnp.sum(p * dp, axis=-1, keepdims=True)) * root).astype(BF)
            acc_q[...] += mm(ds, kh)
            acc_k[...] += mm_tn(ds, qh)
            return carry

        lax.fori_loop(0, 4, head, 0, unroll=4)

    def unnorm(cot, raw, r, gain):
        n = raw * r
        dn = cot.astype(BF).astype(F32) * gain
        inner = head_sum(n * dn, heads[...]) * (1.0 / HD)
        return (r * (dn - n * inner)).astype(BF)

    axes = (
        (x, dev(px=(x + 1) % 4), dev(px=(x - 1) % 4)),
        (y, dev(py=(y + 1) % 4), dev(py=(y - 1) % 4)),
    )

    def ring_send(ref, land, axis, k, copies):
        me, right, left = axes[axis]
        start = (me + k) % 4 * 288
        top, low = ref.at[rows(start, 144)], ref.at[rows(start + 144, 144)]
        if k == 2:
            copies[0] = send(top, land.at[0], right)
            copies[1] = send(low, land.at[1], left)
        elif k == 1:
            copies[2] = send(low, land.at[2], right)
        elif k == 3:
            copies[3] = send(top, land.at[3], left)

    def ring_middle(ref, land, merged, axis, copies):
        me, right, left = axes[axis]
        for i, (at, to) in enumerate((((me + 1) % 4 * 288, right), ((me + 3) % 4 * 288 + 144, left))):
            copies[i].wait_recv()
            merged[i] = (ref[rows(at, 144), :].astype(F32) + land[i].astype(F32)).astype(BF)
            copies.append(send(merged.at[i], land.at[4 + i], to))

    def ring_end(ref, land, axis, copies):
        me = axes[axis][0]
        arrived(copies[2:])
        a = ref[rows(me * 288, 144), :].astype(F32)
        a = a + land[3].astype(F32) + land[4].astype(F32)
        b = ref[rows(me * 288 + 144, 144), :].astype(F32)
        b = b + land[2].astype(F32) + land[5].astype(F32)
        return a.astype(BF), b.astype(BF)

    def sum_middle(g, copies):
        for half, ref in enumerate((g1, g2)):
            ring_middle(ref.at[g], s1.at[g, half], m1.at[g, half], half, copies[half])

    def second_start(g, copies):
        out = []
        for half, (ref, spread) in enumerate(((g1, first), (g2, second))):
            a, b = ring_end(ref.at[g], s1.at[g, half], half, copies[half])
            q1[g, half] = (mm(spread[:, 0:144], a) + mm(spread[:, 144:288], b)).astype(BF)
            if half == 0:
                to = [(flip(*d), dev(py=flip(*d))) for d in flips]
            else:
                to = [((x + dx) % 4, dev(px=(x + dx) % 4)) for dx in (1, 2, 3)]
            out += [
                send(q1.at[g, half, rows(at * 80, 80)], s2.at[g, half, i], target)
                for i, (at, target) in enumerate(to)
            ]
        return out

    def z_start(g, copies):
        arrived(copies)
        total = 0.0
        for half, (spread, me) in enumerate(((upper, y), (lower, x))):
            part = q1[g, half, rows(me * 80, 80), :].astype(F32)
            for i in range(3):
                part = part + s2[g, half, i].astype(F32)
            total = total + mm(spread[...], part.astype(BF))
        zb[g] = total.astype(BF)
        if g == 0:
            return [
                send(zb.at[0, rows((z + dz) % 4 * 48, 48)], zr.at[dz - 1], z_same[dz - 1])
                for dz in (1, 2, 3)
            ]
        return [
            send(zb.at[1, rows((z + dz) % 4 * 48, 48)], zr.at[3 + dz], z_other[dz])
            for dz in range(4)
        ]

    def grads(g):
        gq = unnorm(acc_q[...], qf[...], rq[...], gain_q)
        gk = unnorm(acc_k[...], kf[...], rk[...], gain_k)
        gv = acc_v[...].astype(BF)
        att = acc_o[...].astype(BF)
        pad = jnp.zeros((256, W2 - 2 * HC), BF)
        gx1[...] = jnp.concatenate([gq, gv, pad], axis=1)
        gx2[0:256, :] = jnp.concatenate([gk, jnp.zeros((256, W2 - HC), BF)], axis=1)
        gx2[256:512, :] = jnp.concatenate([jnp.zeros((256, HC), BF), att, pad], axis=1)

        copies = [[None] * 4, [None] * 4]
        for k in (2, 1, 3, 0):
            for half, (ref, left, right) in enumerate(((g1, mod_t, gx1), (g2, both_t, gx2))):
                at = rows((axes[half][0] + k) % 4 * 288, 288)
                ref[g, at, :] = mm(left[at, :], right[...]).astype(BF)
                ring_send(ref.at[g], s1.at[g, half], half, k, copies[half])
        return copies, (gq, gk, gv, att)


    def shares(g, w, parts):
        gq, gk, gv, att = parts
        (q0, q1_), (k0, k1_), (v0, v1_), (o0, o1_) = w(0), w(1), w(2), w(3)
        pieces = (
            (ao, pl.ds(0, W2), mm(att, o0)),
            (ao, pl.ds(W2, W1), mm(att, o1_)),
            (gm, pl.ds(0, W2), mm(gq, q0) + mm(gk, k0) + mm(gv, v0)),
            (gm, pl.ds(W2, W1), mm(gq, q1_) + mm(gk, k1_) + mm(gv, v1_)),
        )
        for ref, at, value in pieces:
            if g == 0:
                ref[:, at] = value
            else:
                ref[:, at] += value

    mod_t[...] = mod[...].T
    both_t[:, 0:256] = mm(turn[...], mod_t[...]).astype(BF)
    forward(own)
    grd3.wait_recv()
    gs[...] = (full[1].astype(F32) * gate).astype(BF)
    both_t[:, 256:512] = mm(turn[...], gs[...].T).astype(BF)
    cotangent(own)
    attention()
    sum_a, made = grads(0)
    shares(0, own, made)
    arrived(w_last)
    forward(other)
    cotangent(other)
    sum_middle(0, sum_a)
    attention()
    sum_b, made = grads(1)
    shares(1, other, made)

    cs[0] = ao[128:256, :].astype(BF)
    cs[1] = gm[128:256, :].astype(BF)
    swapped = [send(cs.at[i], cr.at[i], core) for i in range(2)]
    sum_a = second_start(0, sum_a)
    sum_middle(1, sum_b)

    def back_first(which):
        ob[which] = mm(swap[...], ob[which]).astype(BF)
        block = rows((z * 2 + yh) * 16, 16)
        back[which, block, :] = ob[which, 0:16, :]
        return [
            send(ob.at[which, pl.ds(slot * 16, 16)], back.at[which, block], stage1_from[slot])
            for slot in range(1, 8)
        ]

    def back_last(which):
        backp[which] = mm(swap[...], back[which]).astype(BF)
        block = rows((x * 2 + yl) * 16, 16)
        fin[which, block, :] = backp[which, 0:16, :]
        return [
            send(backp.at[which, pl.ds(slot * 16, 16)], fin.at[which, block], stage2_from[slot])
            for slot in range(1, 8)
        ]

    swapped[0].wait_recv()
    ob[0] = (
        full[0, 0:128, :].astype(F32) + gate * (ao[0:128, :] + cr[0].astype(F32))
    ).astype(BF)
    res_z = back_first(0)
    swapped[1].wait_recv()

    def layer_back(i, carry):
        at = pl.ds(pl.multiple_of(i * 32, 32), 32)
        field = full[0, at, :].astype(F32)
        mean = jnp.mean(field, axis=-1, keepdims=True)
        centred = field - mean
        spread = jnp.mean(centred * centred, axis=-1, keepdims=True)
        r = lax.rsqrt(spread + 1e-06)
        hat = centred * r
        d = (gm[at, :] + cr[1, at, :].astype(F32)) * (1.0 + scale)
        dx = r * (
            d
            - jnp.mean(d, axis=-1, keepdims=True)
            - hat * jnp.mean(d * hat, axis=-1, keepdims=True)
        )
        ob[1, at, :] = (full[1, at, :].astype(F32) + dx).astype(BF)
        return carry

    lax.fori_loop(0, 4, layer_back, 0)
    gin_z = back_first(1)
    sum_a = z_start(0, sum_a)
    sum_b = second_start(1, sum_b)
    arrived(res_z)
    res_xy = back_last(0)
    arrived(gin_z)
    gin_xy = back_last(1)
    sum_b = z_start(1, sum_b)
    arrived(res_xy)
    res_out[...] = mm(swap[...], fin[0]).astype(BF)
    arrived(gin_xy)
    gin_out[...] = mm(swap[...], fin[1]).astype(BF)
    arrived(sum_a)
    arrived(sum_b)
    total = zb[0, rows(z * 48, 48), :].astype(F32)
    for i in range(7):
        total = total + zr[i].astype(F32)
    inproj_out[:, 0, :] = total[0:18, 0:HC]
    inproj_out[:, 1, :] = total[18:36, 0:HC]
    inproj_out[:, 2, :] = total[0:18, HC : 2 * HC]
    outproj_out[...] = total[18:36, HC : 2 * HC]
    for copy in started:
        copy.wait_send()


def place(*refs):
    for i in range(4):
        refs[4 + i][...] = refs[i][...]


N_COPY = 160


def body(tokens_in, mod_shift, mod_scale, branch_gate, inproj, outproj, norm_gain, grad_result):
    swap, turn, first, second, upper, lower, heads = constants()
    vm = pl.BlockSpec(memory_space=pltpu.VMEM)
    anys = pl.BlockSpec(memory_space=pl.ANY)

    def vmem(shape, dtype=BF):
        return pltpu.VMEM(shape, dtype)

    result, grad_in, grad_inproj, grad_outproj = pl.pallas_call(
        kernel,
        out_shape=(
            jax.ShapeDtypeStruct((128, D), BF),
            jax.ShapeDtypeStruct((128, D), BF),
            jax.ShapeDtypeStruct((18, 3, HC), F32),
            jax.ShapeDtypeStruct((18, HC), F32),
        ),
        in_specs=[vm] * 8 + [anys] * 7,
        out_specs=(vm, vm, vm, vm),
        scratch_shapes=[
            vmem((D, D)),
            vmem((D, D)),
            vmem((320, 288)),
            vmem((320, 288)),
            vmem((192, 80)),
            vmem((192, 80)),
            vmem((2, D, W2)),
            *[vmem((128, D))] * 6,
            vmem((2, 256, D)),
            vmem((256, D)),
            vmem((D, 256)),
            vmem((D, 512)),
            vmem((256, D)),
            vmem((256, HC), F32),
            vmem((256, HC), F32),
            vmem((256, HC)),
            vmem((256, HC)),
            vmem((256, HC)),
            vmem((256, HC)),
            vmem((256, HC), F32),
            vmem((256, HC), F32),
            vmem((256, HC), F32),
            vmem((256, HC), F32),
            vmem((256, HC), F32),
            vmem((256, HC), F32),
            vmem((256, D), F32),
            vmem((256, D), F32),
            vmem((256, W2)),
            vmem((512, W2)),
            vmem((2, D, W2)),
            vmem((2, D, W2)),
            vmem((2, 2, 2, 144, W2)),
            vmem((2, 2, 6, 144, W2)),
            vmem((2, 2, 320, W2)),
            vmem((2, 2, 3, 80, W2)),
            vmem((2, 192, W2)),
            vmem((7, 48, W2)),
            vmem((2, 128, D)),
            vmem((2, 128, D)),
            vmem((2, 128, D)),
            vmem((2, 128, D)),
            vmem((2, 128, D)),
            vmem((2, 128, D)),
            pltpu.SemaphoreType.DMA((7,)),
            pltpu.SemaphoreType.DMA((N_COPY,)),
            pltpu.SemaphoreType.DMA((N_COPY,)),
        ],
        compiler_params=pltpu.CompilerParams(
            collective_id=0, has_side_effects=True, vmem_limit_bytes=58 * 2**20
        ),
        name="sublayer",
    )(
        tokens_in, grad_result, mod_shift, mod_scale, branch_gate, norm_gain, swap, heads,
        jnp.transpose(inproj, (1, 2, 0)).reshape(3 * HC, D), outproj,
        turn, first, second, upper, lower,
    )
    made = [result, grad_in, grad_inproj, grad_outproj]
    result, grad_in, grad_inproj, grad_outproj = pl.pallas_call(
        place,
        out_shape=[jax.ShapeDtypeStruct(v.shape, v.dtype) for v in made],
        in_specs=[vm] * 4,
        out_specs=[vm] * 4,
        name="place",
    )(*made)
    return result, grad_in, grad_inproj, grad_outproj.T


def solution(mesh):
    placed = (
        P(("frame", "head"), None),
        P(),
        P(),
        P(),
        P(None, None, "head"),
        P("head", None),
        P(),
        P(("frame", "head"), None),
    )
    return jax.shard_map(
        body,
        mesh=mesh,
        in_specs=placed,
        out_specs=(
            P(("frame", "head"), None),
            P(("frame", "head"), None),
            P("frame", None, "head"),
            P("head", "frame"),
        ),
        check_vma=False,
    )
```

```python
import functools

import jax
import jax.numpy as jnp
import ml_dtypes
import numpy as np
from jax import lax
from jax.experimental import pallas as pl
from jax.experimental.pallas import tpu as pltpu
from jax.sharding import PartitionSpec as P

D = 1152
HD = 72
W2 = 640
W1 = D - W2
HC = 288
BF = jnp.bfloat16
F32 = jnp.float32
MESH = pl.DeviceIdType.MESH

def one_hot(rows, cols, source):
    made = np.zeros((rows, cols), np.float32)
    for row in range(rows):
        col = source(row)
        if col is not None:
            made[row, col] = 1.0
    return made.astype(ml_dtypes.bfloat16)


def constants():
    swap = one_hot(128, 128, lambda o: (o // 2 % 8) * 16 + (o // 16) * 2 + o % 2)
    turn = one_hot(
        D, D, lambda t: (t % 288 // 72) * 288 + (t % 72 // 18) * 72 + (t // 288) * 18 + t % 18
    )
    first = one_hot(
        320,
        288,
        lambda o: (o % 80 // 18) * 72 + (o // 80) * 18 + o % 80 % 18 if o % 80 < 72 else None,
    )
    second = one_hot(320, 288, lambda o: (o // 80) * 72 + o % 80 if o % 80 < 72 else None)
    upper = one_hot(192, 80, lambda o: (o // 48) * 18 + o % 48 if o % 48 < 18 else None)
    lower = one_hot(
        192, 80, lambda o: (o // 48) * 18 + o % 48 - 18 if 18 <= o % 48 < 36 else None
    )
    heads = np.zeros((HC, HC), np.float32)
    for h in range(4):
        heads[h * HD : (h + 1) * HD, h * HD : (h + 1) * HD] = 1.0
    return (swap, turn, first, second, upper, lower, heads.astype(ml_dtypes.bfloat16))


def mm(a, b):
    return jnp.dot(a, b, preferred_element_type=F32)


def mm_nt(a, b):
    return lax.dot_general(a, b, (((1,), (1,)), ((), ())), preferred_element_type=F32)


def mm_tn(a, b):
    return lax.dot_general(a, b, (((0,), (0,)), ((), ())), preferred_element_type=F32)


def head_sum(values, ones):
    high = values.astype(BF)
    low = (values - high.astype(F32)).astype(BF)
    return mm(high, ones) + mm(low, ones)


def kernel(
    tok, grd, shift_in, scale_in, gate_in, gain_in, swap, heads, w_in, w_out, turn_hbm,
    first_hbm, second_hbm, upper_hbm, lower_hbm,
    res_out, gin_out, inproj_out, outproj_out,
    wown, turn, first, second, upper, lower, wo, ta1, ta2, ga1, ga2, ga3, ga4, full, mod, mod_t, both_t, gs, qf, kf, qn, kn, vn, ga, rq, rk,
    acc_o, acc_q, acc_k, acc_v, ao, gm, gx1, gx2, g1, g2, m1, s1, q1, s2, zb, zr, cs, cr,
    ob, back, backp, fin,
    local_sem, ssem, rsem,
):
    f = lax.axis_index("frame")
    h = lax.axis_index("head")
    x, z, yh, yl = f // 16, (f // 4) % 4, (f // 2) % 2, f % 2
    zh, c = h // 2, h % 2
    y = yh * 2 + yl

    def dev(px=x, pz=z, py=y, ph=zh, pc=c):
        return ((px * 4 + pz) * 4 + py, ph * 2 + pc)

    def flip(dh, dl):
        return ((yh + dh) % 2) * 2 + (yl + dl) % 2

    stage1_to = [dev(pz=(z + dz) % 4, py=flip(dh, 0)) for dz in range(4) for dh in range(2)]
    stage1_at = [((z + dz) % 4) * 2 + (yh + dh) % 2 for dz in range(4) for dh in range(2)]
    stage1_from = [dev(pz=(z - dz) % 4, py=flip(dh, 0)) for dz in range(4) for dh in range(2)]
    stage2_to = [dev(px=(x + dx) % 4, py=flip(0, dl)) for dx in range(4) for dl in range(2)]
    stage2_at = [((x + dx) % 4) * 2 + (yl + dl) % 2 for dx in range(4) for dl in range(2)]
    stage2_from = [dev(px=(x - dx) % 4, py=flip(0, dl)) for dx in range(4) for dl in range(2)]
    core = dev(pc=1 - c)
    mirror = dev(pz=3 - z, ph=1 - zh)
    z_other = [dev(pz=(z + dz) % 4, ph=1 - zh) for dz in range(4)]
    z_same = [dev(pz=(z + dz) % 4) for dz in (1, 2, 3)]
    partners = stage1_to[1:] + stage2_to[1:] + [dev(py=flip(1, 1)), core] + z_other

    count = [0]
    started = []

    def send(src, dst, to):
        at = count[0]
        count[0] += 1
        copy = pltpu.make_async_remote_copy(
            src_ref=src, dst_ref=dst, send_sem=ssem.at[at], recv_sem=rsem.at[at],
            device_id=to, device_id_type=MESH,
        )
        copy.start()
        started.append(copy)
        return copy

    def rows(start, size):
        return pl.ds(pl.multiple_of(start, 16), size)

    def arrived(copies):
        for copy in copies:
            copy.wait_recv()

    loads = [
        pltpu.make_async_copy(src, dst, local_sem.at[i])
        for i, (src, dst) in enumerate(
            (
                (w_in, wown.at[pl.ds(0, 864)]),
                (w_out, wown.at[pl.ds(864, HC)]),
                (turn_hbm, turn),
                (first_hbm, first),
                (second_hbm, second),
                (upper_hbm, upper),
                (lower_hbm, lower),
            )
        )
    ]
    for load in loads:
        load.start()

    barrier = pltpu.get_barrier_semaphore()
    for to in partners:
        pl.semaphore_signal(barrier, inc=1, device_id=to, device_id_type=MESH)
    ga1[...] = mm(swap[...], grd[...]).astype(BF)
    loads[0].wait()
    loads[1].wait()
    pl.semaphore_wait(barrier, len(partners))

    def spread(src, dst, places, targets):
        out = []
        for slot in range(8):
            block = rows(places[slot] * 16, 16)
            if slot == 0:
                dst[0:16, :] = src[block, :]
            else:
                out.append(send(src.at[block], dst.at[pl.ds(slot * 16, 16)], targets[slot]))
        return out

    def to_core(which):
        return send(full.at[which, pl.ds(0, 128)], full.at[which, pl.ds(128, 128)], core)

    def piece(px, py):
        return py % 2, (px * 2 + py // 2) * 144

    part, start = piece(x, y)
    lanes = pl.ds(pl.multiple_of(part * 512, 128), W2)
    w_z = [
        send(wown.at[rows(start + at, size), lanes], wo.at[part, rows(start + at, size)], mirror)
        for at, size in ((0, 80), (80, 64))
    ]
    tok1 = spread(tok, ta1, stage1_at, stage1_to)
    grd1 = spread(ga1, ga2, stage2_at, stage2_to)

    flips = ((0, 1), (1, 0), (1, 1))

    def over_x(pc, at, size):
        ref = wo.at[pc, rows(at, size)]
        return [send(ref, ref, dev(px=(x + dx) % 4)) for dx in (1, 2, 3)]

    def over_y(pc, at, size):
        ref = wo.at[pc, rows(at, size)]
        return [send(ref, ref, dev(py=flip(*d))) for d in flips]

    arrived(grd1)
    ga3[...] = mm(swap[...], ga2[...]).astype(BF)
    grd2 = spread(ga3, ga4, stage1_at, stage1_to)
    w_z[0].wait_recv()
    w_x1 = over_x(part, start, 80)
    w_z[1].wait_recv()
    w_y1 = over_y(part, start + 80, 64)
    arrived(tok1)
    ta2[...] = mm(swap[...], ta1[...]).astype(BF)
    tok2 = spread(ta2, full.at[0], stage2_at, stage2_to)
    w_last = over_y(part, start, 80) + over_x(part, start + 80, 64)
    for copy, dx in zip(w_x1, (1, 2, 3)):
        copy.wait_recv()
        pc, at = piece((x - dx) % 4, y)
        w_last += over_y(pc, at, 80)
    for copy, d in zip(w_y1, flips):
        copy.wait_recv()
        pc, at = piece(x, flip(*d))
        w_last += over_x(pc, at + 80, 64)
    shift = shift_in[...].reshape(1, D)
    scale = scale_in[...].reshape(1, D)
    gate = gate_in[...].reshape(1, D)

    def modulate(i, carry):
        at = pl.ds(pl.multiple_of(i * 32, 32), 32)
        field = full[0, at, :].astype(F32)
        mean = jnp.mean(field, axis=-1, keepdims=True)
        centred = field - mean
        spread = jnp.mean(centred * centred, axis=-1, keepdims=True)
        mod[at, :] = (centred * lax.rsqrt(spread + 1e-06) * (1.0 + scale) + shift).astype(BF)
        return carry

    arrived(tok2)
    tok3 = to_core(0)
    arrived(grd2)
    full[1, 0:128, :] = mm(swap[...], ga4[...]).astype(BF)
    grd3 = to_core(1)
    lax.fori_loop(0, 4, modulate, 0)
    tok3.wait_recv()
    lax.fori_loop(4, 8, modulate, 0)
    for load in loads[2:]:
        load.wait()

    lane = lax.broadcasted_iota(jnp.int32, (1, HC), 1)
    row_i = lax.broadcasted_iota(jnp.int32, (256, 256), 0)
    col_i = lax.broadcasted_iota(jnp.int32, (256, 256), 1)
    gain_q = jnp.concatenate([gain_in[0:1, :]] * 4, axis=1)
    gain_k = jnp.concatenate([gain_in[1:2, :]] * 4, axis=1)

    def own(j):
        at = pl.ds(j * HC, HC)
        return wown[at, 0:W2], wown[at, W2:D]

    def other(j):
        at = pl.ds(j * HC, HC)
        return wo[0, at, :], wo[1, at, W2 - W1 : W2]

    def project(act, w, j):
        low, high = w(j)
        return mm_nt(act[:, 0:W2], low) + mm_nt(act[:, W2:D], high)

    def forward(w):
        q = project(mod, w, 0)
        qf[...] = q
        r = lax.rsqrt(head_sum(q * q, heads[...]) * (1.0 / HD) + 1e-06)
        rq[...] = r
        qn[...] = (q * r * gain_q).astype(BF)
        k = project(mod, w, 1)
        kf[...] = k
        r = lax.rsqrt(head_sum(k * k, heads[...]) * (1.0 / HD) + 1e-06)
        rk[...] = r
        kn[...] = (k * r * gain_k).astype(BF)
        vn[...] = project(mod, w, 2).astype(BF)

    def cotangent(w):
        ga[...] = project(gs, w, 3).astype(BF)

    def attention():
        acc_o[...] = jnp.zeros_like(acc_o)
        acc_q[...] = jnp.zeros_like(acc_q)
        acc_k[...] = jnp.zeros_like(acc_k)
        acc_v[...] = jnp.zeros_like(acc_v)
        same = (row_i // 128 == col_i // 128) & (row_i % 2 == col_i % 2)
        root = 1.0 / np.sqrt(np.float32(HD))

        def head(i, carry):
            inside = (lane >= i * HD) & (lane < i * HD + HD)
            zero = jnp.zeros((), BF)
            qh = jnp.where(inside, qn[...], zero)
            kh = jnp.where(inside, kn[...], zero)
            vh = jnp.where(inside, vn[...], zero)
            gh = jnp.where(inside, ga[...], zero)
            s = jnp.where(same, mm_nt(qh, kh) * root, -1e30)
            e = jnp.exp(s - jnp.max(s, axis=-1, keepdims=True))
            p = e * (1.0 / jnp.sum(e, axis=-1, keepdims=True))
            pb = p.astype(BF)
            acc_o[...] += mm(pb, vh)
            acc_v[...] += mm_tn(pb, gh)
            dp = mm_nt(gh, vh)
            ds = (p * (dp - jnp.sum(p * dp, axis=-1, keepdims=True)) * root).astype(BF)
            acc_q[...] += mm(ds, kh)
            acc_k[...] += mm_tn(ds, qh)
            return carry

        lax.fori_loop(0, 4, head, 0, unroll=4)

    def unnorm(cot, raw, r, gain):
        n = raw * r
        dn = cot.astype(BF).astype(F32) * gain
        inner = head_sum(n * dn, heads[...]) * (1.0 / HD)
        return (r * (dn - n * inner)).astype(BF)

    axes = (
        (x, dev(px=(x + 1) % 4), dev(px=(x - 1) % 4)),
        (y, dev(py=(y + 1) % 4), dev(py=(y - 1) % 4)),
    )

    def ring_send(ref, land, axis, k, copies):
        me, right, left = axes[axis]
        start = (me + k) % 4 * 288
        top, low = ref.at[rows(start, 144)], ref.at[rows(start + 144, 144)]
        if k == 2:
            copies[0] = send(top, land.at[0], right)
            copies[1] = send(low, land.at[1], left)
        elif k == 1:
            copies[2] = send(low, land.at[2], right)
        elif k == 3:
            copies[3] = send(top, land.at[3], left)

    def ring_middle(ref, land, merged, axis, copies):
        me, right, left = axes[axis]
        for i, (at, to) in enumerate((((me + 1) % 4 * 288, right), ((me + 3) % 4 * 288 + 144, left))):
            copies[i].wait_recv()
            merged[i] = (ref[rows(at, 144), :].astype(F32) + land[i].astype(F32)).astype(BF)
            copies.append(send(merged.at[i], land.at[4 + i], to))

    def ring_end(ref, land, axis, copies):
        me = axes[axis][0]
        arrived(copies[2:])
        a = ref[rows(me * 288, 144), :].astype(F32)
        a = a + land[3].astype(F32) + land[4].astype(F32)
        b = ref[rows(me * 288 + 144, 144), :].astype(F32)
        b = b + land[2].astype(F32) + land[5].astype(F32)
        return a.astype(BF), b.astype(BF)

    def sum_middle(g, copies):
        for half, ref in enumerate((g1, g2)):
            ring_middle(ref.at[g], s1.at[g, half], m1.at[g, half], half, copies[half])

    def second_start(g, copies):
        out = []
        for half, (ref, spread) in enumerate(((g1, first), (g2, second))):
            a, b = ring_end(ref.at[g], s1.at[g, half], half, copies[half])
            q1[g, half] = (mm(spread[:, 0:144], a) + mm(spread[:, 144:288], b)).astype(BF)
            if half == 0:
                to = [(flip(*d), dev(py=flip(*d))) for d in flips]
            else:
                to = [((x + dx) % 4, dev(px=(x + dx) % 4)) for dx in (1, 2, 3)]
            out += [
                send(q1.at[g, half, rows(at * 80, 80)], s2.at[g, half, i], target)
                for i, (at, target) in enumerate(to)
            ]
        return out

    def z_start(g, copies):
        arrived(copies)
        total = 0.0
        for half, (spread, me) in enumerate(((upper, y), (lower, x))):
            part = q1[g, half, rows(me * 80, 80), :].astype(F32)
            for i in range(3):
                part = part + s2[g, half, i].astype(F32)
            total = total + mm(spread[...], part.astype(BF))
        zb[g] = total.astype(BF)
        if g == 0:
            return [
                send(zb.at[0, rows((z + dz) % 4 * 48, 48)], zr.at[dz - 1], z_same[dz - 1])
                for dz in (1, 2, 3)
            ]
        return [
            send(zb.at[1, rows((z + dz) % 4 * 48, 48)], zr.at[3 + dz], z_other[dz])
            for dz in range(4)
        ]

    def grads(g):
        gq = unnorm(acc_q[...], qf[...], rq[...], gain_q)
        gk = unnorm(acc_k[...], kf[...], rk[...], gain_k)
        gv = acc_v[...].astype(BF)
        att = acc_o[...].astype(BF)
        pad = jnp.zeros((256, W2 - 2 * HC), BF)
        gx1[...] = jnp.concatenate([gq, gv, pad], axis=1)
        gx2[0:256, :] = jnp.concatenate([gk, jnp.zeros((256, W2 - HC), BF)], axis=1)
        gx2[256:512, :] = jnp.concatenate([jnp.zeros((256, HC), BF), att, pad], axis=1)

        copies = [[None] * 4, [None] * 4]
        for k in (2, 1, 3, 0):
            for half, (ref, left, right) in enumerate(((g1, mod_t, gx1), (g2, both_t, gx2))):
                at = rows((axes[half][0] + k) % 4 * 288, 288)
                ref[g, at, :] = mm(left[at, :], right[...]).astype(BF)
                ring_send(ref.at[g], s1.at[g, half], half, k, copies[half])
        return copies, (gq, gk, gv, att)


    def shares(g, w, parts):
        gq, gk, gv, att = parts
        (q0, q1_), (k0, k1_), (v0, v1_), (o0, o1_) = w(0), w(1), w(2), w(3)
        pieces = (
            (ao, pl.ds(0, W2), mm(att, o0)),
            (ao, pl.ds(W2, W1), mm(att, o1_)),
            (gm, pl.ds(0, W2), mm(gq, q0) + mm(gk, k0) + mm(gv, v0)),
            (gm, pl.ds(W2, W1), mm(gq, q1_) + mm(gk, k1_) + mm(gv, v1_)),
        )
        for ref, at, value in pieces:
            if g == 0:
                ref[:, at] = value
            else:
                ref[:, at] += value

    mod_t[...] = mod[...].T
    both_t[:, 0:256] = mm(turn[...], mod_t[...]).astype(BF)
    forward(own)
    grd3.wait_recv()
    gs[...] = (full[1].astype(F32) * gate).astype(BF)
    both_t[:, 256:512] = mm(turn[...], gs[...].T).astype(BF)
    cotangent(own)
    attention()
    sum_a, made = grads(0)
    shares(0, own, made)
    arrived(w_last)
    forward(other)
    cotangent(other)
    sum_middle(0, sum_a)
    attention()
    sum_b, made = grads(1)
    shares(1, other, made)

    cs[0] = ao[128:256, :].astype(BF)
    cs[1] = gm[128:256, :].astype(BF)
    swapped = [send(cs.at[i], cr.at[i], core) for i in range(2)]
    sum_a = second_start(0, sum_a)
    sum_middle(1, sum_b)

    def back_first(which):
        ob[which] = mm(swap[...], ob[which]).astype(BF)
        block = rows((z * 2 + yh) * 16, 16)
        back[which, block, :] = ob[which, 0:16, :]
        return [
            send(ob.at[which, pl.ds(slot * 16, 16)], back.at[which, block], stage1_from[slot])
            for slot in range(1, 8)
        ]

    def back_last(which):
        backp[which] = mm(swap[...], back[which]).astype(BF)
        block = rows((x * 2 + yl) * 16, 16)
        fin[which, block, :] = backp[which, 0:16, :]
        return [
            send(backp.at[which, pl.ds(slot * 16, 16)], fin.at[which, block], stage2_from[slot])
            for slot in range(1, 8)
        ]

    swapped[0].wait_recv()
    ob[0] = (
        full[0, 0:128, :].astype(F32) + gate * (ao[0:128, :] + cr[0].astype(F32))
    ).astype(BF)
    res_z = back_first(0)
    swapped[1].wait_recv()

    def layer_back(i, carry):
        at = pl.ds(pl.multiple_of(i * 32, 32), 32)
        field = full[0, at, :].astype(F32)
        mean = jnp.mean(field, axis=-1, keepdims=True)
        centred = field - mean
        spread = jnp.mean(centred * centred, axis=-1, keepdims=True)
        r = lax.rsqrt(spread + 1e-06)
        hat = centred * r
        d = (gm[at, :] + cr[1, at, :].astype(F32)) * (1.0 + scale)
        dx = r * (
            d
            - jnp.mean(d, axis=-1, keepdims=True)
            - hat * jnp.mean(d * hat, axis=-1, keepdims=True)
        )
        ob[1, at, :] = (full[1, at, :].astype(F32) + dx).astype(BF)
        return carry

    lax.fori_loop(0, 4, layer_back, 0)
    gin_z = back_first(1)
    sum_a = z_start(0, sum_a)
    sum_b = second_start(1, sum_b)
    arrived(res_z)
    res_xy = back_last(0)
    sum_b = z_start(1, sum_b)
    arrived(gin_z)
    gin_xy = back_last(1)
    arrived(res_xy)
    res_out[...] = mm(swap[...], fin[0]).astype(BF)
    arrived(gin_xy)
    gin_out[...] = mm(swap[...], fin[1]).astype(BF)
    arrived(sum_a)
    arrived(sum_b)
    total = zb[0, rows(z * 48, 48), :].astype(F32)
    for i in range(7):
        total = total + zr[i].astype(F32)
    inproj_out[:, 0, :] = total[0:18, 0:HC]
    inproj_out[:, 1, :] = total[18:36, 0:HC]
    inproj_out[:, 2, :] = total[0:18, HC : 2 * HC]
    outproj_out[...] = total[18:36, HC : 2 * HC]
    for copy in started:
        copy.wait_send()


def place(*refs):
    for i in range(4):
        refs[4 + i][...] = refs[i][...]


N_COPY = 160


def body(tokens_in, mod_shift, mod_scale, branch_gate, inproj, outproj, norm_gain, grad_result):
    swap, turn, first, second, upper, lower, heads = constants()
    vm = pl.BlockSpec(memory_space=pltpu.VMEM)
    anys = pl.BlockSpec(memory_space=pl.ANY)

    def vmem(shape, dtype=BF):
        return pltpu.VMEM(shape, dtype)

    result, grad_in, grad_inproj, grad_outproj = pl.pallas_call(
        kernel,
        out_shape=(
            jax.ShapeDtypeStruct((128, D), BF),
            jax.ShapeDtypeStruct((128, D), BF),
            jax.ShapeDtypeStruct((18, 3, HC), F32),
            jax.ShapeDtypeStruct((18, HC), F32),
        ),
        in_specs=[vm] * 8 + [anys] * 7,
        out_specs=(vm, vm, vm, vm),
        scratch_shapes=[
            vmem((D, D)),
            vmem((D, D)),
            vmem((320, 288)),
            vmem((320, 288)),
            vmem((192, 80)),
            vmem((192, 80)),
            vmem((2, D, W2)),
            *[vmem((128, D))] * 6,
            vmem((2, 256, D)),
            vmem((256, D)),
            vmem((D, 256)),
            vmem((D, 512)),
            vmem((256, D)),
            vmem((256, HC), F32),
            vmem((256, HC), F32),
            vmem((256, HC)),
            vmem((256, HC)),
            vmem((256, HC)),
            vmem((256, HC)),
            vmem((256, HC), F32),
            vmem((256, HC), F32),
            vmem((256, HC), F32),
            vmem((256, HC), F32),
            vmem((256, HC), F32),
            vmem((256, HC), F32),
            vmem((256, D), F32),
            vmem((256, D), F32),
            vmem((256, W2)),
            vmem((512, W2)),
            vmem((2, D, W2)),
            vmem((2, D, W2)),
            vmem((2, 2, 2, 144, W2)),
            vmem((2, 2, 6, 144, W2)),
            vmem((2, 2, 320, W2)),
            vmem((2, 2, 3, 80, W2)),
            vmem((2, 192, W2)),
            vmem((7, 48, W2)),
            vmem((2, 128, D)),
            vmem((2, 128, D)),
            vmem((2, 128, D)),
            vmem((2, 128, D)),
            vmem((2, 128, D)),
            vmem((2, 128, D)),
            pltpu.SemaphoreType.DMA((7,)),
            pltpu.SemaphoreType.DMA((N_COPY,)),
            pltpu.SemaphoreType.DMA((N_COPY,)),
        ],
        compiler_params=pltpu.CompilerParams(
            collective_id=0, has_side_effects=True, vmem_limit_bytes=58 * 2**20
        ),
        name="sublayer",
    )(
        tokens_in, grad_result, mod_shift, mod_scale, branch_gate, norm_gain, swap, heads,
        jnp.transpose(inproj, (1, 2, 0)).reshape(3 * HC, D), outproj,
        turn, first, second, upper, lower,
    )
    made = [result, grad_in, grad_inproj, grad_outproj]
    result, grad_in, grad_inproj, grad_outproj = pl.pallas_call(
        place,
        out_shape=[jax.ShapeDtypeStruct(v.shape, v.dtype) for v in made],
        in_specs=[vm] * 4,
        out_specs=[vm] * 4,
        name="place",
    )(*made)
    return result, grad_in, grad_inproj, grad_outproj.T


def solution(mesh):
    placed = (
        P(("frame", "head"), None),
        P(),
        P(),
        P(),
        P(None, None, "head"),
        P("head", None),
        P(),
        P(("frame", "head"), None),
    )
    return jax.shard_map(
        body,
        mesh=mesh,
        in_specs=placed,
        out_specs=(
            P(("frame", "head"), None),
            P(("frame", "head"), None),
            P("frame", None, "head"),
            P("head", "frame"),
        ),
        check_vma=False,
    )
```
